32 devices in a mesh: samp: 16 (over z, x, core), blk: 2 (over y).
Axes of the slice: x: 2, y: 2, z: 4, core: 2. Of those that a mesh axis runs over, the one named last changes fastest.
Arguments:
- genotypes: bfloat16 [16384, 1000], P('samp', 'blk'), may hold values from 0 to 2, as said below
- traits: float32 [16384, 8], P('samp'), may hold values from -3000 to 3000
- observed: int32 [16384, 8], P('samp'), may hold values from 0 to 1, as said below
- fold_index: int32 [16384], P('samp'), may hold values from 0 to 4, never falling along the last dimension, each value on 1 to 6553 neighbouring positions
Outputs:
- stack_gram: float32 [8, 5, 10, 10], P('blk')
- stack_cross: float32 [8, 5, 10], P('blk')
The draws below stay inside these ranges and needn't reach their ends.
Inputs may be any that keep to these rules, and one draw needn't show every extreme that they name: `genotypes`: genotype dosages, whole numbers. `observed`: each trait is measured in at least one sample.
All inputs are finite; a program needn't handle non-finite values.
Results may differ from the reference program's by a relative error of at most 0.0003.
Values sent between devices are 32-bit elements; how exact they have to be, the bound alone decides.
No kernel may reach another device: no remote copies, remote signals or barrier semaphores. Data moves between devices by JAX's collectives and lax.ppermute only.
A program may use at most 64 MiB of HBM per device.

```python
import math
import jax
import jax.numpy as jnp
import numpy as np
from jax import lax

BLOCK = 500
TRAITS = 8
FOLDS = 5
SAMPLES = 16384
BLOCKS = 2
SNPS = 1000


def dosage_draw(key):
    base_key = jax.random.fold_in(key, 11)
    freq_key, allele_key, link_key = jax.random.split(base_key, 3)
    baseline = jax.random.randint(freq_key, (SNPS,), 20, 334)
    row_ids = jnp.arange(SAMPLES, dtype=jnp.int32)
    threshold = baseline[None, :] * (SAMPLES + 2 * row_ids[:, None]) // SAMPLES
    dice_rolls = jax.random.randint(allele_key, (SAMPLES, SNPS), 0, 10000000)
    first_allele = (dice_rolls % 1000 < threshold).astype(jnp.int32)
    second_allele = (dice_rolls // 1000 % 1000 < threshold).astype(jnp.int32)
    fresh = first_allele + second_allele
    link_level = jax.random.randint(link_key, (SNPS,), 5, 10)
    snp_ids = jnp.arange(SNPS, dtype=jnp.int32)
    linked = jnp.logical_and(dice_rolls // 1000000 < link_level[None, :], snp_ids[None, :] > 0)
    run_start = jnp.where(linked, 0, snp_ids[None, :]).astype(jnp.int32)
    source = lax.cummax(run_start, axis=1)
    return jnp.take_along_axis(fresh, source, axis=1)


def draw_genotypes(key, part):
    return dosage_draw(key).astype(jnp.float32).astype(jnp.bfloat16)


def draw_traits(key, part):
    dosage = dosage_draw(key)
    trait_key = jax.random.fold_in(key, 23)
    sub_keys = jax.random.split(trait_key, 5)
    effects = jax.random.randint(sub_keys[0], (SNPS, TRAITS), -1, 2)
    signal = jnp.dot(dosage, effects).astype(jnp.float32)
    genetic = jnp.clip(signal / math.sqrt(0.25 * SNPS), -6.0, 6.0)
    heritability = jax.random.uniform(sub_keys[1], (TRAITS,), minval=0.2, maxval=0.8)
    trait_scale = jnp.exp(jax.random.uniform(sub_keys[2], (TRAITS,), minval=0.0, maxval=math.log(10.0)))
    position = jnp.arange(SAMPLES, dtype=jnp.float32) / (SAMPLES - 1)
    row_scale = jnp.exp(math.log(10.0) * position)[:, None]
    trait_shift = jax.random.uniform(sub_keys[3], (TRAITS,), minval=-3.0, maxval=3.0)
    noise_part = jnp.clip(jax.random.normal(sub_keys[4], (SAMPLES, TRAITS)), -4.0, 4.0)
    mixture = jnp.sqrt(heritability) * genetic + jnp.sqrt(1.0 - heritability) * noise_part
    return (trait_shift + trait_scale * row_scale * mixture).astype(jnp.float32)


def draw_observed(key, part):
    base_key = jax.random.fold_in(key, 37)
    keep_key, roll_key = jax.random.split(base_key)
    keep_level = jax.random.randint(keep_key, (TRAITS,), 5, 10)
    dice_rolls = jax.random.randint(roll_key, (SAMPLES, TRAITS), 0, 10)
    first_row = (jnp.arange(SAMPLES, dtype=jnp.int32) == 0)[:, None]
    measured = (dice_rolls < keep_level[None, :]).astype(jnp.int32)
    return jnp.where(first_row, 1, measured).astype(jnp.int32)


def profile(amount, total, bound, lean):
    portions = [(1 << 20) // math.isqrt(grade ** lean) + 1 for grade in range(2, amount + 1)]
    rest, holding = total - bound - (amount - 1), [1] * (amount - 1)
    while rest > 0:
        movable = [i for i in range(amount - 1) if holding[i] < bound]
        mass, left = sum([portions[i] for i in movable]), rest
        for i in movable:
            extra = min(bound - holding[i], max(1, left * portions[i] // mass), rest)
            holding[i] = holding[i] + extra
            rest = rest - extra
    return np.array([bound] + holding)


def uneven_parts(stream_key, count, total, limit, slope):
    if count == 2:
        one = jax.random.randint(stream_key, (), max(1, total - limit), min(limit, total - 1) + 1)
        return jnp.stack([one, total - one])
    tallies = jnp.asarray(profile(count, total, limit, slope), jnp.int32)
    couples = (count - 1) // 2
    giver, taker = tallies[1:1 + 2 * couples:2], tallies[2:2 + 2 * couples:2]
    room = jnp.minimum(giver - 1, limit - taker)
    moved = jax.random.randint(jax.random.fold_in(stream_key, 1), (couples,), 0, 1 << 20) % (room + 1)
    tallies = tallies.at[1:1 + 2 * couples:2].set(giver - moved).at[2:2 + 2 * couples:2].set(taker + moved)
    return tallies[jax.random.permutation(jax.random.fold_in(stream_key, 2), count)]


def setup_inputs(seed: int = 0) -> dict:
    streams_of = jax.random.split(jax.random.key(seed), 5)
    return {
        "genotypes": draw_genotypes(jax.random.fold_in(streams_of[4], 71), 0),
        "traits": draw_traits(jax.random.fold_in(streams_of[4], 71), 0),
        "observed": draw_observed(jax.random.fold_in(streams_of[4], 71), 0),
        "fold_index": jnp.searchsorted(jnp.cumsum(uneven_parts(streams_of[3], FOLDS, SAMPLES, 2 * SAMPLES // FOLDS, 1)), jnp.arange(SAMPLES), side="right").astype(jnp.int32),
    }


HERITABILITY = (0.01, 0.25, 0.5, 0.75, 0.99)
PRECISE = lax.Precision.HIGHEST

def reference(genotypes, traits, observed, fold_index):
    present = observed.astype(jnp.float32)
    masked = present * traits
    counts = lax.optimization_barrier(jnp.sum(present, 0))
    mean_trait = lax.optimization_barrier(jnp.sum(masked, 0)) / counts
    trait_scale = jnp.sqrt(lax.optimization_barrier(jnp.sum(masked * traits, 0)) / counts - mean_trait * mean_trait + 1e-05)
    scaled = present * (traits - mean_trait) / trait_scale
    identity = jnp.eye(BLOCK, dtype=jnp.float32)
    columns = []
    for block_index in range(BLOCKS):
        dosage = genotypes[:, block_index * BLOCK:(block_index + 1) * BLOCK].astype(jnp.float32)
        gram_block = jnp.dot(dosage.T, dosage, precision=PRECISE)
        column_sums = lax.optimization_barrier(jnp.sum(dosage, 0))
        mean_dosage = column_sums / SAMPLES
        dosage_scale = jnp.sqrt(jnp.diagonal(gram_block) / SAMPLES - mean_dosage * mean_dosage + 1e-05)
        covariance = (gram_block - column_sums[:, None] * column_sums[None, :] / SAMPLES) / (dosage_scale[:, None] * dosage_scale[None, :])
        dosage_trait = jnp.dot(dosage.T, masked, precision=PRECISE)
        dosage_present = jnp.dot(dosage.T, present, precision=PRECISE)
        right_side = (dosage_trait - dosage_present * mean_trait) / trait_scale / dosage_scale[:, None]
        centred = (dosage - mean_dosage) / dosage_scale
        for fraction in HERITABILITY:
            lower_factor = jnp.linalg.cholesky(covariance + SNPS * (1.0 - fraction) / fraction * identity)
            solution = jax.scipy.linalg.cho_solve((lower_factor, True), right_side)
            predicted = jnp.dot(centred, solution, precision=PRECISE)
            energy = lax.optimization_barrier(jnp.sum(predicted * predicted, 0))
            columns.append(predicted / jnp.sqrt(energy / SAMPLES + 1e-06))
    standard = jnp.stack(columns, 2)
    fold_hits = (fold_index[None, :] == jnp.arange(FOLDS, dtype=jnp.int32)[:, None]).astype(jnp.float32)
    gram_list = []
    cross_list = []
    for trait_index in range(TRAITS):
        stacked = standard[:, trait_index, :]
        weighting = fold_hits * present[:, trait_index][None, :]
        weighted = weighting[:, :, None] * stacked[None]
        gram_sum = jnp.einsum('ksl,sm->klm', weighted, stacked, precision=PRECISE)
        cross_sum = jnp.einsum('ksl,s->kl', weighted, scaled[:, trait_index], precision=PRECISE)
        gram_list.append(gram_sum * (FOLDS / SAMPLES))
        cross_list.append(cross_sum * (FOLDS / SAMPLES))
    return (jnp.stack(gram_list, 0), jnp.stack(cross_list, 0))
```

```python
import functools
import jax
import jax.numpy as jnp
from jax import lax
from jax.experimental import pallas as pl
from jax.experimental.pallas import tpu as pltpu
from jax.sharding import PartitionSpec as P

TRAITS = 8
FOLDS = 5
HERITABILITY = (0.01, 0.25, 0.5, 0.75, 0.99)
TILE = 128
STEP = 8
SIDE = 32
SLOTS = 6
HALF = SLOTS // 2
VMEM_BYTES = 32 * 1024 * 1024

NN = (((1,), (0,)), ((), ()))
NT = (((1,), (1,)), ((), ()))
TN = (((0,), (0,)), ((), ()))


def dot(a, b, dims=NN):
    return lax.dot_general(
        a, b, dims, precision=lax.Precision.HIGHEST, preferred_element_type=jnp.float32
    )


def dot_bf16(a, b, dims=NN):
    return lax.dot_general(a, b, dims, preferred_element_type=jnp.float32)


def split_three(value):
    high = value.astype(jnp.bfloat16)
    left = value - high.astype(jnp.float32)
    middle = left.astype(jnp.bfloat16)
    low = (left - middle.astype(jnp.float32)).astype(jnp.bfloat16)
    return high, middle, low


def iota(shape, dim):
    return lax.broadcasted_iota(jnp.int32, shape, dim)


def block_rows(tiles):
    place, row = {}, 0
    for i in range(tiles):
        for j in range(i, tiles):
            place[i, j] = row
            row += TILE
    return place, row


def call(kernel, out_shape, in_specs, scratch, name):
    vmem = pl.BlockSpec(memory_space=pltpu.VMEM)
    smem = pl.BlockSpec(memory_space=pltpu.SMEM)
    return pl.pallas_call(
        kernel,
        out_shape=out_shape,
        in_specs=[smem if spec == "smem" else vmem if spec == "vmem" else spec for spec in in_specs],
        out_specs=jax.tree.map(lambda _: vmem, out_shape),
        scratch_shapes=scratch,
        compiler_params=pltpu.CompilerParams(vmem_limit_bytes=VMEM_BYTES),
        name=name,
    )


def gram_kernel(markers, dosage, traits, observed, packed, padded):
    width, rows = padded.shape
    tiles = width // TILE
    place, side = block_rows(tiles)
    edge = markers // 16 * 16
    padded[0:edge, :] = dosage[0:edge, :]
    tail = dosage[edge:edge + 16, :].astype(jnp.float32)
    tail = jnp.where(iota(tail.shape, 0) + edge < markers, tail, 0.0)
    padded[edge:edge + 16, :] = tail.astype(jnp.bfloat16)
    if edge + 16 < width:
        padded[edge + 16:, :] = jnp.zeros((width - edge - 16, rows), jnp.bfloat16)
    values = traits[...]
    present = observed[...].astype(jnp.float32)
    masked = present * values
    high, middle, low = (part.astype(jnp.float32) for part in split_three(masked))
    ones = jnp.ones(present.shape, jnp.float32)
    extra = jnp.concatenate([high, middle, low, present, ones, ones], 0).astype(jnp.bfloat16)
    products = dot_bf16(extra, padded[...], NT)
    sums = [jnp.sum(v, axis=1, keepdims=True) for v in (present, masked, masked * values)]
    lane = iota((TRAITS, TILE), 1)
    stats = jnp.where(
        lane == 0, sums[0], jnp.where(lane == 1, sums[1], jnp.where(lane == 2, sums[2], 0.0))
    )
    for i in range(tiles):
        here = dot_bf16(padded[i * TILE:(i + 1) * TILE, :], padded[i * TILE:, :], NT)
        for j in range(i, tiles):
            packed[place[i, j]:place[i, j] + TILE, :] = here[:, (j - i) * TILE:(j - i + 1) * TILE]
        cols = slice(i * TILE, (i + 1) * TILE)
        row = side + SIDE * i
        packed[row:row + 8, :] = products[0:8, cols] + products[8:16, cols] + products[16:24, cols]
        packed[row + 8:row + 16, :] = products[24:32, cols]
        packed[row + 16:row + 24, :] = products[32:40, cols]
        packed[row + 24:row + 32, :] = stats


def eliminate(work, old, fits):
    shape = (fits, STEP, TILE)
    row, lane = iota(shape, 1), iota(shape, 2)
    count = TILE // STEP
    for t in range(count):
        base = t * STEP
        panel = work[:, base:base + STEP, :]
        cols = [
            jnp.broadcast_to(panel[:, :, base + m:base + m + 1], shape) for m in range(STEP)
        ]
        inside = jnp.logical_and(lane >= base, lane < base + STEP)
        panel = jnp.where(inside, jnp.where(lane - base == row, 1.0, 0.0), panel)
        old[:, base:base + STEP, :] = jnp.where(lane < base + STEP, panel, 0.0)
        scale = None
        for j in range(STEP):
            inverse = jnp.broadcast_to(1.0 / cols[j][:, j:j + 1, :], shape)
            here = row == j
            gain = jnp.where(here, 0.0, cols[j] * inverse)
            scale = inverse if scale is None else jnp.where(here, inverse, scale)
            for m in range(j + 1, STEP):
                cols[m] = cols[m] - gain * cols[m][:, j:j + 1, :]
            panel = panel - gain * panel[:, j:j + 1, :]
        panel = panel * scale
        work[:, base:base + STEP, :] = panel
        rows = [jnp.broadcast_to(panel[:, q:q + 1, :], shape) for q in range(STEP)]
        for g in range(t + 1, count):
            other = work[:, g * STEP:(g + 1) * STEP, :]
            total = jnp.where(inside, 0.0, other)
            for q in range(STEP):
                total = total - jnp.broadcast_to(
                    other[:, :, base + q:base + q + 1], shape
                ) * rows[q]
            work[:, g * STEP:(g + 1) * STEP, :] = total


def fit_kernel(samples, markers, penalty, packed, out, stats, centre, grid, wide, work, old, rhs):
    fits = work.shape[0]
    tiles = rhs.shape[-1] // TILE
    place, side = block_rows(tiles)

    def part(tile, which):
        row = side + SIDE * tile + 8 * which
        return packed[row:row + 8, :]

    sums = part(0, 3)
    counts, first, second = sums[:, 0:1], sums[:, 1:2], sums[:, 2:3]
    mean = first / counts
    spread = jnp.sqrt(second / counts - mean * mean + 1e-05)
    lane = iota((TRAITS, TILE), 1)
    stats[...] = jnp.where(lane == 0, mean, jnp.where(lane == 1, spread, 0.0))
    eye = iota((TILE, TILE), 0) == iota((TILE, TILE), 1)
    lower = iota((TILE, TILE), 1) // STEP <= iota((TILE, TILE), 0) // STEP
    line = iota((1, TILE), 1)
    share = 1.0 / samples
    totals = [part(i, 2)[0:1, :] for i in range(tiles)]
    columns = [jnp.transpose(jnp.broadcast_to(t, (TILE, TILE))) for t in totals]
    squares = []
    for i in range(tiles):
        mine = slice(i * TILE, (i + 1) * TILE)
        block = packed[place[i, i]:place[i, i] + TILE, :]
        diagonal = jnp.sum(jnp.where(eye, block, 0.0), axis=0, keepdims=True)
        middle = totals[i] * share
        centre[:, mine] = jnp.broadcast_to(middle, (8, TILE))
        squares.append(diagonal * share - middle * middle + 1e-05)
        for j in range(i, tiles):
            block = packed[place[i, j]:place[i, j] + TILE, :]
            grid[i, :, j * TILE:(j + 1) * TILE] = block - columns[i] * totals[j] * share
        side_i = (part(i, 0) - part(i, 1) * mean) / spread
        for f in range(fits):
            rhs[f, :, mine] = side_i

    def ridge(i, f):
        value = jnp.where(line + i * TILE < markers, penalty[f] * squares[i], 1.0)
        return jnp.where(eye, value, 0.0)

    for k in range(tiles):
        lo, hi = k * TILE, (k + 1) * TILE
        for f in range(fits):
            work[f] = grid[0, :, lo:hi] + ridge(0, f) if k == 0 else wide[f, k, :, lo:hi]
        eliminate(work, old, fits)
        for f in range(fits):
            inverse = dot(old[f], jnp.where(lower, work[f], 0.0), TN)
            mine = rhs[f, :, lo:hi]
            rhs[f, :, lo:hi] = dot(mine, inverse)
            if hi == tiles * TILE:
                continue
            above = grid[0, :, hi:] if k == 0 else wide[f, k, :, hi:]
            weights = dot(inverse, above)
            rhs[f, :, hi:] = rhs[f, :, hi:] - dot(mine, weights)
            for i in range(k + 1, tiles):
                begin = i * TILE
                before = grid[i, :, begin:] if k == 0 else wide[f, i, :, begin:]
                column = above[:, begin - hi:begin - hi + TILE]
                wide[f, i, :, begin:] = before - dot(column, weights[:, begin - hi:], TN)
                if k == 0:
                    wide[f, i, :, begin:begin + TILE] = wide[f, i, :, begin:begin + TILE] + ridge(i, f)
            wide[f, k, :, hi:] = weights
    for f in range(fits):
        for k in reversed(range(tiles)):
            lo, hi = k * TILE, (k + 1) * TILE
            value = rhs[f, :, lo:hi]
            if hi < tiles * TILE:
                value = value - dot(out[f, :, hi:], wide[f, k, :, hi:], NT)
            out[f, :, lo:hi] = value


def predict_kernel(pairs, place, mine, other, centre, padded, out):
    odd = place[0] == 1
    rows = []
    for f in range(HALF):
        rows.append(jnp.where(odd, other[f], mine[f]))
    for f in range(HALF):
        rows.append(jnp.where(odd, mine[f], other[f]))
    if pairs:
        upper = iota(rows[0].shape, 0) < TRAITS // 2
        second = place[1] == 1
        halves = [[], []]
        for s in range(0, SLOTS, 2):
            a, b = rows[s], rows[s + 1]
            turned_a, turned_b = (pltpu.roll(v, TRAITS // 2, 0) for v in (a, b))
            low, high = jnp.where(upper, a, turned_b), jnp.where(upper, turned_a, b)
            halves[0].append(jnp.where(second, high, low))
            halves[1].append(jnp.where(second, low, high))
        rows = halves[0] + halves[1]
    weights = jnp.concatenate(rows, 0)
    count = weights.shape[0]
    shift = jnp.sum(weights * centre[0:1, :], axis=1, keepdims=True)
    parts = [part.astype(jnp.float32) for part in split_three(weights)]
    product = dot_bf16(jnp.concatenate(parts, 0).astype(jnp.bfloat16), padded[...])
    total = product[0:count] + product[count:2 * count] + product[2 * count:3 * count] - shift
    if pairs:
        out[0] = total[:count // 2]
        out[1] = total[count // 2:]
    else:
        out[...] = total


def stack_kernel(pairs, per_share, place, mine, other, stats, traits, observed, folds, out):
    first = place[1] * per_share
    if pairs:
        second = place[1] == 1
        levels = jnp.concatenate(
            [jnp.where(second, other[...], mine[...]), jnp.where(second, mine[...], other[...])], 0
        )
    else:
        levels = mine[...]
    count, samples = levels.shape
    present = observed[...].astype(jnp.float32)
    scaled = present * (traits[...] - stats[:, 0:1]) / stats[:, 1:2]
    pick = iota((count, TRAITS), 1) == first + iota((count, TRAITS), 0) % per_share
    spread = dot_bf16(
        jnp.where(pick, 1.0, 0.0).astype(jnp.bfloat16), present.astype(jnp.bfloat16)
    )
    kept = levels * spread
    left = [kept * jnp.where(folds[...] == k, 1.0, 0.0) for k in range(FOLDS)] + [levels]
    left = jnp.concatenate(left, 0)
    right = jnp.concatenate([levels, scaled], 0)
    full = dot(right, left, NT)
    row, col = iota(full.shape, 0), iota(full.shape, 1)
    trait = jnp.where(row < count, row % per_share, row - count - first)
    full = jnp.where(trait == col % per_share, full, 0.0)
    shape = (out.shape[0], full.shape[0])
    level, source = iota(shape, 0), iota(shape, 1)
    group = jnp.where(source < count, source // per_share, count // per_share)
    out[...] = dot(jnp.where(level == group, 1.0, 0.0), full)


def scale_kernel(per_share, samples, total, out):
    height, width = total.shape
    count = width // (FOLDS + 1)
    value = total[...]
    level, column = iota((height, count), 0), iota((height, count), 1)
    energy = jnp.where(level == column // per_share, value[:, FOLDS * count:], 0.0)
    shape = (count, width)
    source, target = iota(shape, 0), iota(shape, 1)
    by_row = dot(energy, jnp.where(source % per_share == target % per_share, 1.0, 0.0))
    every = jnp.broadcast_to(jnp.sum(energy, axis=0, keepdims=True), (8, count))
    by_column = dot(every, jnp.where(source == target % count, 1.0, 0.0))[0:1, :]
    root_row = jnp.where(
        iota((height, width), 0) < count // per_share, jnp.sqrt(by_row / samples + 1e-06), 1.0
    )
    root_column = jnp.sqrt(by_column / samples + 1e-06)
    out[...] = value / root_row / root_column * (FOLDS / samples)


def swap(value, axis, mask):
    size = lax.axis_size(axis)
    return lax.ppermute(value, axis, [(i, i ^ mask) for i in range(size)])


def masks_of(axis):
    size, mask, found = lax.axis_size(axis), 1, []
    while mask < size:
        found.append(mask)
        mask *= 2
    return found


def sum_over(value, axis, halvings):
    masks = masks_of(axis)
    position = lax.axis_index(axis)
    for mask in masks[:halvings]:
        half = value.shape[0] // 2
        low, high = value[:half], value[half:]
        up = (position & mask) != 0
        value = jnp.where(up, high, low) + swap(jnp.where(up, low, high), axis, mask)
    for mask in masks[halvings:]:
        value = value + swap(value, axis, mask)
    for mask in reversed(masks[:halvings]):
        up = (position & mask) != 0
        other = swap(value, axis, mask)
        value = jnp.concatenate([jnp.where(up, other, value), jnp.where(up, value, other)], 0)
    return value


def body(genotypes, traits, observed, fold_index):
    local_rows, markers = genotypes.shape
    sample_devices = lax.axis_size("samp")
    block_devices = lax.axis_size("blk")
    samples = local_rows * sample_devices
    all_markers = markers * block_devices
    width = -(-markers // TILE) * TILE
    tiles = width // TILE
    per_share = TRAITS // block_devices
    pairs = block_devices == 2
    f32 = functools.partial(jax.ShapeDtypeStruct, dtype=jnp.float32)
    position, block = lax.axis_index("samp"), lax.axis_index("blk")
    odd = position % 2
    place = jnp.stack([odd, block]).astype(jnp.int32)
    traits, observed = traits.T, observed.T
    _, side = block_rows(tiles)

    whole = lambda shape: pl.BlockSpec(shape, lambda _: (0, 0))
    packed, padded = pl.pallas_call(
        functools.partial(gram_kernel, markers),
        grid=(1,),
        out_shape=[
            f32((side + SIDE * tiles, TILE)),
            jax.ShapeDtypeStruct((width, local_rows), jnp.bfloat16),
        ],
        in_specs=[whole((width, local_rows)), whole(traits.shape), whole(observed.shape)],
        out_specs=[whole((side + SIDE * tiles, TILE)), whole((width, local_rows))],
        compiler_params=pltpu.CompilerParams(vmem_limit_bytes=VMEM_BYTES),
        name="local_gram",
    )(genotypes.T, traits, observed)
    packed = sum_over(packed, "samp", 2)

    penalties = [all_markers * (1.0 - h) / h for h in HERITABILITY]
    penalties = penalties + [penalties[-1]] * (SLOTS - len(penalties))
    penalty = jnp.where(
        odd == 1,
        jnp.array(penalties[HALF:], jnp.float32),
        jnp.array(penalties[:HALF], jnp.float32),
    )
    weights, stats, centre = call(
        functools.partial(fit_kernel, samples, markers),
        [f32((HALF, TRAITS, width)), f32((TRAITS, TILE)), f32((8, width))],
        ["smem", "vmem"],
        [
            pltpu.VMEM((tiles, TILE, width), jnp.float32),
            pltpu.VMEM((HALF, tiles, TILE, width), jnp.float32),
            pltpu.VMEM((HALF, TILE, TILE), jnp.float32),
            pltpu.VMEM((HALF, TILE, TILE), jnp.float32),
            pltpu.VMEM((HALF, TRAITS, width), jnp.float32),
        ],
        "ridge_fits",
    )(penalty, packed)
    other = swap(weights, "samp", 1)

    count = SLOTS * TRAITS
    shape = (2, count // 2, local_rows) if pairs else (count, local_rows)
    predicted = call(
        functools.partial(predict_kernel, pairs),
        f32(shape),
        ["smem", "vmem", "vmem", "vmem", "vmem"],
        [],
        "predictions",
    )(place, weights, other, centre, padded)
    if pairs:
        mine, theirs = predicted[0], swap(predicted[1], "blk", 1)
    else:
        shares = predicted.reshape(SLOTS, block_devices, per_share, local_rows)
        shares = lax.all_to_all(shares, "blk", split_axis=1, concat_axis=0, tiled=True)
        mine = theirs = shares.reshape(count, local_rows)

    levels = count // per_share
    height = -(-(levels + 1) // 8) * 8
    products = call(
        functools.partial(stack_kernel, pairs, per_share),
        f32((height, (FOLDS + 1) * count)),
        ["smem"] + ["vmem"] * 6,
        [],
        "stacking",
    )(place, mine, theirs, stats, traits, observed, fold_index[None, :])
    products = sum_over(products, "samp", 0)
    result = call(
        functools.partial(scale_kernel, per_share, samples),
        f32((height, (FOLDS + 1) * count)),
        ["vmem"],
        [],
        "standardize",
    )(products)

    fits = len(HERITABILITY)
    result = result[:, :FOLDS * count].reshape(height, FOLDS, block_devices, SLOTS, per_share)
    result = result[:, :, :, :fits, :].reshape(height, FOLDS, block_devices * fits, per_share)
    gram = result[:levels].reshape((block_devices, SLOTS) + result.shape[1:])[:, :fits]
    gram = gram.reshape((block_devices * fits,) + result.shape[1:])
    return gram.transpose(3, 1, 2, 0), result[levels].transpose(2, 0, 1)


def solution(mesh):
    in_specs = (P("samp", "blk"), P("samp", None), P("samp", None), P("samp"))
    out_specs = (P("blk", None, None, None), P("blk", None, None))
    return jax.shard_map(body, mesh=mesh, in_specs=in_specs, out_specs=out_specs, check_vma=False)
```

```python
import functools
import jax
import jax.numpy as jnp
from jax import lax
from jax.experimental import pallas as pl
from jax.experimental.pallas import tpu as pltpu
from jax.sharding import PartitionSpec as P

TRAITS = 8
FOLDS = 5
HERITABILITY = (0.01, 0.25, 0.5, 0.75, 0.99)
TILE = 128
STEP = 8
SIDE = 24
SUB = 32
FITS = len(HERITABILITY)
SLOTS = 6
HALF = SLOTS // 2
VMEM_BYTES = 32 * 1024 * 1024

NN = (((1,), (0,)), ((), ()))
NT = (((1,), (1,)), ((), ()))
TN = (((0,), (0,)), ((), ()))


def dot(a, b, dims=NN):
    return lax.dot_general(
        a, b, dims, precision=lax.Precision.HIGHEST, preferred_element_type=jnp.float32
    )


def dot_bf16(a, b, dims=NN):
    return lax.dot_general(a, b, dims, preferred_element_type=jnp.float32)


def split_three(value):
    high = value.astype(jnp.bfloat16)
    left = value - high.astype(jnp.float32)
    middle = left.astype(jnp.bfloat16)
    low = (left - middle.astype(jnp.float32)).astype(jnp.bfloat16)
    return high, middle, low


def iota(shape, dim):
    return lax.broadcasted_iota(jnp.int32, shape, dim)


def dot_six(a, b, dims=NN):
    if dims == TN:
        a, dims = jnp.transpose(a), NN
    (along_a,), (along_b,) = dims[0]
    high_a, middle_a, low_a = split_three(a)
    high_b, middle_b, low_b = split_three(b)

    def part(x, y):
        return dot_bf16(jnp.concatenate(x, along_a), jnp.concatenate(y, along_b), dims)

    small = part([low_a, middle_a], [high_b, middle_b])
    return (small + part([middle_a, high_a], [high_b, middle_b])) + part(
        [high_a, high_a], [low_b, high_b]
    )


def block_rows(tiles):
    place, row = {}, 0
    for i in range(tiles):
        for j in range(i + 1, tiles):
            place[i, j] = row
            row += TILE
    for i in range(0, tiles, 2):
        place[i, i] = place[i + 1, i + 1] = row
        row += TILE
    return place, row


def call(kernel, out_shape, in_specs, scratch, name):
    vmem = pl.BlockSpec(memory_space=pltpu.VMEM)
    smem = pl.BlockSpec(memory_space=pltpu.SMEM)
    return pl.pallas_call(
        kernel,
        out_shape=out_shape,
        in_specs=[smem if spec == "smem" else vmem for spec in in_specs],
        out_specs=jax.tree.map(lambda _: vmem, out_shape),
        scratch_shapes=scratch,
        compiler_params=pltpu.CompilerParams(vmem_limit_bytes=VMEM_BYTES),
        name=name,
    )


def gram_kernel(markers, dosage, traits, observed, packed, padded):
    width, rows = padded.shape
    tiles = width // TILE
    place, side = block_rows(tiles)
    edge = markers // 16 * 16
    padded[0:edge, :] = dosage[0:edge, :]
    tail = dosage[edge:edge + 16, :].astype(jnp.float32)
    tail = jnp.where(iota(tail.shape, 0) + edge < markers, tail, 0.0)
    padded[edge:edge + 16, :] = tail.astype(jnp.bfloat16)
    if edge + 16 < width:
        padded[edge + 16:, :] = jnp.zeros((width - edge - 16, rows), jnp.bfloat16)
    values = traits[...]
    present = observed[...].astype(jnp.float32)
    masked = present * values
    high, middle, low = (part.astype(jnp.float32) for part in split_three(masked))
    ones = jnp.ones(present.shape, jnp.float32)
    extra = jnp.concatenate([high, middle, low, present, ones, ones], 0).astype(jnp.bfloat16)
    products = dot_bf16(extra, padded[...], NT)
    sums = [jnp.sum(v, axis=1, keepdims=True) for v in (present, masked, masked * values)]
    lane, line = iota((TRAITS, TILE), 1), iota((TRAITS, TILE), 0)
    upper = iota((TILE, TILE), 0) <= iota((TILE, TILE), 1)
    eye = iota((TILE, TILE), 0) == iota((TILE, TILE), 1)
    even = None
    for i in range(tiles):
        here = dot_bf16(padded[i * TILE:(i + 1) * TILE, :], padded[i * TILE:, :], NT)
        for j in range(i + 1, tiles):
            packed[place[i, j]:place[i, j] + TILE, :] = here[:, (j - i) * TILE:(j - i + 1) * TILE]
        block = here[:, :TILE]
        if i % 2:
            packed[place[i, i]:place[i, i] + TILE, :] = jnp.where(upper, even, block)
        even = block
        diagonal = jnp.sum(jnp.where(eye, block, 0.0), axis=0, keepdims=True)
        cols = slice(i * TILE, (i + 1) * TILE)
        row = side + SIDE * i
        total = products[0:8, cols] + products[8:16, cols] + products[16:24, cols]
        if i == tiles - 1:
            for n, value in enumerate(sums):
                total = jnp.where(lane == TILE - 1 - n, value, total)
        packed[row:row + 8, :] = total
        packed[row + 8:row + 16, :] = products[24:32, cols]
        packed[row + 16:row + 24, :] = jnp.where(line == 0, products[32:40, cols], diagonal)


def eliminate(work, old, fits):
    shape = (fits, STEP, TILE)
    row, lane = iota(shape, 1), iota(shape, 2)
    count, per = TILE // STEP, SUB // STEP
    for t in range(count):
        base = t * STEP
        panel = work[:, base:base + STEP, :]
        cols = [
            jnp.broadcast_to(panel[:, :, base + m:base + m + 1], shape) for m in range(STEP)
        ]
        inside = jnp.logical_and(lane >= base, lane < base + STEP)
        panel = jnp.where(inside, jnp.where(lane - base == row, 1.0, 0.0), panel)
        old[:, base:base + STEP, :] = panel
        scale = None
        for j in range(STEP):
            inverse = jnp.broadcast_to(1.0 / cols[j][:, j:j + 1, :], shape)
            here = row == j
            gain = jnp.where(here, 0.0, cols[j] * inverse)
            scale = inverse if scale is None else jnp.where(here, inverse, scale)
            for m in range(j + 1, STEP):
                cols[m] = cols[m] - gain * cols[m][:, j:j + 1, :]
            panel = panel - gain * panel[:, j:j + 1, :]
        panel = panel * scale
        work[:, base:base + STEP, :] = panel
        rows = [jnp.broadcast_to(panel[:, q:q + 1, :], shape) for q in range(STEP)]
        stop = (t // per + 1) * per
        for g in range(t + 1, stop):
            other = work[:, g * STEP:(g + 1) * STEP, :]
            total = jnp.where(inside, 0.0, other)
            for q in range(STEP):
                total = total - jnp.broadcast_to(
                    other[:, :, base + q:base + q + 1], shape
                ) * rows[q]
            work[:, g * STEP:(g + 1) * STEP, :] = total
        if t + 1 == stop and stop < count:
            first, last = (t + 1 - per) * STEP, stop * STEP
            line, column = iota((SUB, TILE), 0) + first, iota((SUB, TILE), 1)
            keep = jnp.logical_or(column >= last, column // STEP <= line // STEP)
            column = iota((TILE - last, TILE), 1)
            done = jnp.logical_and(column >= first, column < last)
            for f in range(fits):
                left = split_three(old[f, first:last, :])
                right = split_three(jnp.where(keep, work[f, first:last, :], 0.0))
                product = dot_bf16(
                    jnp.concatenate([left[i] for i in (0, 0, 0, 1, 1, 2)], 0),
                    jnp.concatenate([right[i] for i in (0, 1, 2, 0, 1, 0)], 0),
                    TN,
                )
                rest = work[f, last:, :]
                work[f, last:, :] = jnp.where(done, 0.0, rest) - product[last:, :]
    lower = iota(old.shape, 2) // STEP <= iota(old.shape, 1) // STEP
    old[...] = jnp.where(lower, old[...], 0.0)
    work[...] = jnp.where(lower, work[...], 0.0)


def fit_kernel(samples, markers, penalty, packed, out, stats, centre, grid, wide, work, old, rhs):
    fits = work.shape[0]
    tiles = rhs.shape[-1] // TILE
    end = tiles * TILE
    place, side = block_rows(tiles)

    def part(tile, which):
        row = side + SIDE * tile + 8 * which
        return packed[row:row + 8, :]

    sums = part(tiles - 1, 0)
    counts, first, second = (sums[:, TILE - 1 - n:TILE - n] for n in range(3))
    mean = first / counts
    spread = jnp.sqrt(second / counts - mean * mean + 1e-05)
    lane = iota((TRAITS, TILE), 1)
    stats[...] = jnp.where(lane == 0, mean, jnp.where(lane == 1, spread, 0.0))
    row, col = iota((TILE, TILE), 0), iota((TILE, TILE), 1)
    eye, upper = row == col, row <= col
    line = iota((1, TILE), 1)
    share = 1.0 / samples
    totals = [part(i, 2)[0:1, :] for i in range(tiles)]
    squares = []
    for i in range(tiles):
        mine = slice(i * TILE, (i + 1) * TILE)
        column = jnp.transpose(jnp.broadcast_to(totals[i], (TILE, TILE)))
        diagonal = part(i, 2)[1:2, :]
        middle = totals[i] * share
        centre[:, mine] = jnp.broadcast_to(middle, (8, TILE))
        squares.append(diagonal * share - middle * middle + 1e-05)
        for j in range(i, tiles):
            block = packed[place[i, j]:place[i, j] + TILE, :]
            if i == j:
                turned = jnp.transpose(block)
                if i % 2:
                    block = jnp.where(upper, turned, block)
                    block = jnp.where(eye, diagonal, block)
                else:
                    block = jnp.where(upper, block, turned)
            grid[i, :, j * TILE:(j + 1) * TILE] = block - column * totals[j] * share
        side_i = (part(i, 0) - part(i, 1) * mean) / spread
        if i == tiles - 1:
            side_i = jnp.where(lane + i * TILE < markers, side_i, 0.0)
        for f in range(fits):
            rhs[f, :, mine] = side_i

    def ridge(i, f):
        value = jnp.where(line + i * TILE < markers, penalty[f] * squares[i], 1.0)
        return jnp.where(eye, value, 0.0)

    for f in range(fits):
        work[f] = grid[0, :, 0:TILE] + ridge(0, f)
    for k in range(tiles):
        lo, hi = k * TILE, (k + 1) * TILE
        eliminate(work, old, fits)
        lefts, rights = [old[f] for f in range(fits)], [work[f] for f in range(fits)]
        both = None
        if hi < end:
            above = [grid[0, :, hi:] if k == 0 else wide[f, k, :, hi:] for f in range(fits)]
            both = [
                dot_six(jnp.concatenate([lefts[f], rights[f]], 0), above[f]) for f in range(fits)
            ]
        for i in range(k + 1, tiles):
            for f in range(fits):
                begin = i * TILE
                left, weights = both[f][:TILE, begin - hi:begin - hi + TILE], both[f][TILE:, begin - hi:]
                before = grid[i, :, begin:] if k == 0 else wide[f, i, :, begin:]
                after = before - dot_six(left, weights, TN)
                block = after[:, :TILE] + ridge(i, f) if k == 0 else after[:, :TILE]
                if i == k + 1:
                    work[f] = block
                else:
                    wide[f, i, :, begin:begin + TILE] = block
                if i + 1 < tiles:
                    wide[f, i, :, begin + TILE:] = after[:, TILE:]
        for f in range(fits):
            turned = dot(rhs[f, :, lo:hi], lefts[f], NT)
            rhs[f, :, lo:hi] = dot(turned, rights[f])
            if hi < end:
                weights = both[f][TILE:]
                rhs[f, :, hi:] = rhs[f, :, hi:] - dot(turned, weights)
                wide[f, k, :, hi:] = dot_six(lefts[f], weights, TN)
    for k in reversed(range(tiles)):
        for f in range(fits):
            lo, hi = k * TILE, (k + 1) * TILE
            value = rhs[f, :, lo:hi]
            if hi < end:
                value = value - dot(out[f, :, hi:], wide[f, k, :, hi:], NT)
            out[f, :, lo:hi] = value


def predict_kernel(pairs, place, mine, other, centre, padded, out):
    odd = place[0] == 1
    rows = []
    for f in range(HALF):
        rows.append(jnp.where(odd, other[f], mine[f]))
    for f in range(HALF):
        rows.append(jnp.where(odd, mine[f], other[f]))
    if pairs:
        upper = iota(rows[0].shape, 0) < TRAITS // 2
        second = place[1] == 1
        halves = [[], []]
        for s in range(0, SLOTS, 2):
            a, b = rows[s], rows[s + 1]
            turned_a, turned_b = (pltpu.roll(v, TRAITS // 2, 0) for v in (a, b))
            low, high = jnp.where(upper, a, turned_b), jnp.where(upper, turned_a, b)
            halves[0].append(jnp.where(second, high, low))
            halves[1].append(jnp.where(second, low, high))
        rows = halves[0] + halves[1]
    weights = jnp.concatenate(rows, 0)
    count = weights.shape[0]
    shift = jnp.sum(weights * centre[0:1, :], axis=1, keepdims=True)
    parts = [part.astype(jnp.float32) for part in split_three(weights)]
    product = dot_bf16(jnp.concatenate(parts, 0).astype(jnp.bfloat16), padded[...])
    total = product[0:count] + product[count:2 * count] + product[2 * count:3 * count] - shift
    if pairs:
        out[0] = total[:count // 2]
        out[1] = total[count // 2:]
    else:
        out[...] = total


def stack_kernel(pairs, per_share, place, mine, other, stats, traits, observed, folds, out):
    first = place[1] * per_share
    if pairs:
        second = place[1] == 1
        levels = jnp.concatenate(
            [jnp.where(second, other[...], mine[...]), jnp.where(second, mine[...], other[...])], 0
        )
    else:
        levels = mine[...]
    count, samples = levels.shape
    height, width = out.shape
    present = observed[...].astype(jnp.float32)
    scaled = present * (traits[...] - stats[:, 0:1]) / stats[:, 1:2]
    pick = iota((count, TRAITS), 1) == first + iota((count, TRAITS), 0) % per_share
    spread = dot_bf16(
        jnp.where(pick, 1.0, 0.0).astype(jnp.bfloat16), present.astype(jnp.bfloat16)
    )
    kept = levels * spread
    left = [kept * jnp.where(folds[...] == k, 1.0, 0.0) for k in range(FOLDS)]
    left = left + [jnp.zeros((width - FOLDS * count, samples), jnp.float32)]
    left = jnp.concatenate(left, 0)
    right = jnp.concatenate([levels, scaled], 0)
    full = dot(right, left, NT)
    row, col = iota(full.shape, 0), iota(full.shape, 1)
    trait = jnp.where(row < count, row % per_share, row - count - first)
    full = jnp.where(trait == col % per_share, full, 0.0)
    shape = (height, full.shape[0])
    level, source = iota(shape, 0), iota(shape, 1)
    slot = source // per_share
    group = jnp.where(slot % SLOTS < FITS, slot // SLOTS * FITS + slot % SLOTS, height)
    group = jnp.where(source < count, group, count // per_share // SLOTS * FITS)
    out[...] = dot(jnp.where(level == group, 1.0, 0.0), full)
    energy = dot(jnp.ones((8, samples), jnp.float32), levels * levels, NT)
    last = count // per_share // SLOTS * FITS + 1
    out[last:last + 1, 0:count] = energy[0:1, :]


def scale_kernel(per_share, blocks, samples, total, gram, cross):
    height, width = total.shape
    count = blocks * SLOTS * per_share
    levels = blocks * FITS
    value = total[...]
    energy = jnp.broadcast_to(value[levels + 1:levels + 2, 0:count], (height, count))
    level, column = iota((height, count), 0), iota((height, count), 1) // per_share
    group = jnp.where(column % SLOTS < FITS, column // SLOTS * FITS + column % SLOTS, height)
    shape = (count, width)
    source, target = iota(shape, 0), iota(shape, 1)
    by_row = dot(
        jnp.where(level == group, energy, 0.0),
        jnp.where(source % per_share == target % per_share, 1.0, 0.0),
    )
    by_column = dot(energy, jnp.where(source == target % count, 1.0, 0.0))
    root_row = jnp.where(
        iota((height, width), 0) < levels, jnp.sqrt(by_row / samples + 1e-06), 1.0
    )
    root_column = jnp.sqrt(by_column / samples + 1e-06)
    value = value / root_row / root_column * (FOLDS / samples)
    turned = jnp.transpose(value)
    shape = (FOLDS * 8, width)
    line, column = iota(shape, 0), iota(shape, 1)
    chosen = jnp.logical_and(line // 8 == column // count, line % 8 == column % per_share)
    products = jnp.where(chosen, jnp.broadcast_to(value[levels:levels + 1, :], shape), 0.0)
    shape = (width, TILE)
    slot, target = iota(shape, 0) % count // per_share, iota(shape, 1)
    group = jnp.where(slot % SLOTS < FITS, slot // SLOTS * FITS + slot % SLOTS, -1)
    products = dot(products, jnp.where(group == target, 1.0, 0.0))
    for k in range(FOLDS):
        cross[k] = products[8 * k:8 * k + per_share, 0:levels]
        for l in range(levels):
            row = k * count + (l // FITS * SLOTS + l % FITS) * per_share
            gram[k, l] = turned[row:row + per_share, 0:levels]


def swap(value, axis, mask):
    size = lax.axis_size(axis)
    return lax.ppermute(value, axis, [(i, i ^ mask) for i in range(size)])


def masks_of(axis):
    size, mask, found = lax.axis_size(axis), 1, []
    while mask < size:
        found.append(mask)
        mask *= 2
    return found


def sum_over(value, axis, halvings):
    masks = masks_of(axis)
    position = lax.axis_index(axis)
    for mask in masks[:halvings]:
        half = value.shape[0] // 2
        low, high = value[:half], value[half:]
        up = (position & mask) != 0
        value = jnp.where(up, high, low) + swap(jnp.where(up, low, high), axis, mask)
    for mask in masks[halvings:]:
        value = value + swap(value, axis, mask)
    for mask in reversed(masks[:halvings]):
        up = (position & mask) != 0
        other = swap(value, axis, mask)
        value = jnp.concatenate([jnp.where(up, other, value), jnp.where(up, value, other)], 0)
    return value


def body(genotypes, traits, observed, fold_index):
    local_rows, markers = genotypes.shape
    sample_devices = lax.axis_size("samp")
    block_devices = lax.axis_size("blk")
    samples = local_rows * sample_devices
    all_markers = markers * block_devices
    width = -(-markers // TILE) * TILE
    tiles = width // TILE
    per_share = TRAITS // block_devices
    pairs = block_devices == 2
    f32 = functools.partial(jax.ShapeDtypeStruct, dtype=jnp.float32)
    position, block = lax.axis_index("samp"), lax.axis_index("blk")
    odd = position % 2
    place = jnp.stack([odd, block]).astype(jnp.int32)
    traits, observed = traits.T, observed.T
    _, side = block_rows(tiles)

    whole = lambda shape: pl.BlockSpec(shape, lambda _: (0, 0))
    packed, padded = pl.pallas_call(
        functools.partial(gram_kernel, markers),
        grid=(1,),
        out_shape=[
            f32((side + SIDE * tiles, TILE)),
            jax.ShapeDtypeStruct((width, local_rows), jnp.bfloat16),
        ],
        in_specs=[whole((width, local_rows)), whole(traits.shape), whole(observed.shape)],
        out_specs=[whole((side + SIDE * tiles, TILE)), whole((width, local_rows))],
        compiler_params=pltpu.CompilerParams(vmem_limit_bytes=VMEM_BYTES),
        name="local_gram",
    )(genotypes.T, traits, observed)
    packed = sum_over(packed, "samp", 2)

    penalties = [all_markers * (1.0 - h) / h for h in HERITABILITY]
    penalties = penalties + [penalties[-1]] * (SLOTS - len(penalties))
    penalty = jnp.where(
        odd == 1,
        jnp.array(penalties[HALF:], jnp.float32),
        jnp.array(penalties[:HALF], jnp.float32),
    )
    weights, stats, centre = call(
        functools.partial(fit_kernel, samples, markers),
        [f32((HALF, TRAITS, width)), f32((TRAITS, TILE)), f32((8, width))],
        ["smem", "vmem"],
        [
            pltpu.VMEM((tiles, TILE, width), jnp.float32),
            pltpu.VMEM((HALF, tiles, TILE, width), jnp.float32),
            pltpu.VMEM((HALF, TILE, TILE), jnp.float32),
            pltpu.VMEM((HALF, TILE, TILE), jnp.float32),
            pltpu.VMEM((HALF, TRAITS, width), jnp.float32),
        ],
        "ridge_fits",
    )(penalty, packed)
    other = swap(weights, "samp", 1)

    count = SLOTS * TRAITS
    shape = (2, count // 2, local_rows) if pairs else (count, local_rows)
    predicted = call(
        functools.partial(predict_kernel, pairs),
        f32(shape),
        ["smem", "vmem", "vmem", "vmem", "vmem"],
        [],
        "predictions",
    )(place, weights, other, centre, padded)
    if pairs:
        mine, theirs = predicted[0], swap(predicted[1], "blk", 1)
    else:
        shares = predicted.reshape(SLOTS, block_devices, per_share, local_rows)
        shares = lax.all_to_all(shares, "blk", split_axis=1, concat_axis=0, tiled=True)
        mine = theirs = shares.reshape(count, local_rows)

    levels = block_devices * FITS
    height = -(-(levels + 2) // 8) * 8
    lanes = -(-FOLDS * count // TILE) * TILE
    products = call(
        functools.partial(stack_kernel, pairs, per_share),
        f32((height, lanes)),
        ["smem"] + ["vmem"] * 6,
        [],
        "stacking",
    )(place, mine, theirs, stats, traits, observed, fold_index[None, :])
    products = sum_over(products, "samp", 0)
    gram, cross = call(
        functools.partial(scale_kernel, per_share, block_devices, samples),
        [f32((FOLDS, levels, per_share, levels)), f32((FOLDS, per_share, levels))],
        ["vmem"],
        [],
        "standardize",
    )(products)
    return gram.transpose(2, 0, 1, 3), cross.transpose(1, 0, 2)


def solution(mesh):
    in_specs = (P("samp", "blk"), P("samp", None), P("samp", None), P("samp"))
    out_specs = (P("blk", None, None, None), P("blk", None, None))
    return jax.shard_map(body, mesh=mesh, in_specs=in_specs, out_specs=out_specs, check_vma=False)
```

```python
import functools
import jax
import jax.numpy as jnp
from jax import lax
from jax.experimental import pallas as pl
from jax.experimental.pallas import tpu as pltpu
from jax.sharding import PartitionSpec as P

TRAITS = 8
FOLDS = 5
HERITABILITY = (0.01, 0.25, 0.5, 0.75, 0.99)
TILE = 128
STEP = 8
SIDE = 24
SUB = 32
FITS = len(HERITABILITY)
SLOTS = 6
HALF = SLOTS // 2
VMEM_BYTES = 32 * 1024 * 1024

NN = (((1,), (0,)), ((), ()))
NT = (((1,), (1,)), ((), ()))
TN = (((0,), (0,)), ((), ()))


def dot(a, b, dims=NN):
    return lax.dot_general(
        a, b, dims, precision=lax.Precision.HIGHEST, preferred_element_type=jnp.float32
    )


def dot_bf16(a, b, dims=NN):
    return lax.dot_general(a, b, dims, preferred_element_type=jnp.float32)


def split_three(value):
    high = value.astype(jnp.bfloat16)
    left = value - high.astype(jnp.float32)
    middle = left.astype(jnp.bfloat16)
    low = (left - middle.astype(jnp.float32)).astype(jnp.bfloat16)
    return high, middle, low


def iota(shape, dim):
    return lax.broadcasted_iota(jnp.int32, shape, dim)


def left_parts(value):
    high, middle, low = split_three(value)
    return [jnp.concatenate(pair, 1) for pair in ((low, middle), (middle, high), (high, high))]


def right_parts(value):
    high, middle, low = split_three(value)
    first = jnp.concatenate([high, middle], 0)
    return [first, first, jnp.concatenate([low, high], 0)]


def products(lefts, rights):
    totals = [dot_bf16(a[0], b[0]) for a, b in zip(lefts, rights)]
    for part in (1, 2):
        terms = [dot_bf16(a[part], b[part]) for a, b in zip(lefts, rights)]
        totals = [total + term for total, term in zip(totals, terms)]
    return totals


def block_rows(tiles):
    place, row = {}, 0
    for i in range(tiles):
        for j in range(i + 1, tiles):
            place[i, j] = row
            row += TILE
    for i in range(0, tiles, 2):
        place[i, i] = place[i + 1, i + 1] = row
        row += TILE
    return place, row


def call(kernel, out_shape, in_specs, scratch, name):
    vmem = pl.BlockSpec(memory_space=pltpu.VMEM)
    smem = pl.BlockSpec(memory_space=pltpu.SMEM)
    return pl.pallas_call(
        kernel,
        out_shape=out_shape,
        in_specs=[smem if spec == "smem" else vmem for spec in in_specs],
        out_specs=jax.tree.map(lambda _: vmem, out_shape),
        scratch_shapes=scratch,
        compiler_params=pltpu.CompilerParams(vmem_limit_bytes=VMEM_BYTES),
        name=name,
    )


def gram_kernel(markers, dosage, traits, observed, packed, padded, held, seen, arrived):
    copies = [
        pltpu.make_async_copy(traits, held, arrived.at[0]),
        pltpu.make_async_copy(observed, seen, arrived.at[1]),
    ]
    for copy in copies:
        copy.start()
    width, rows = padded.shape
    tiles = width // TILE
    place, side = block_rows(tiles)
    edge = markers // 16 * 16
    padded[0:edge, :] = dosage[0:edge, :]
    tail = dosage[edge:edge + 16, :].astype(jnp.float32)
    tail = jnp.where(iota(tail.shape, 0) + edge < markers, tail, 0.0)
    padded[edge:edge + 16, :] = tail.astype(jnp.bfloat16)
    if edge + 16 < width:
        padded[edge + 16:, :] = jnp.zeros((width - edge - 16, rows), jnp.bfloat16)
    lane, line = iota((TRAITS, TILE), 1), iota((TRAITS, TILE), 0)
    upper = iota((TILE, TILE), 0) <= iota((TILE, TILE), 1)
    eye = iota((TILE, TILE), 0) == iota((TILE, TILE), 1)
    even, diagonals = None, []
    for i in range(tiles):
        here = dot_bf16(padded[i * TILE:(i + 1) * TILE, :], padded[i * TILE:, :], NT)
        for j in range(i + 1, tiles):
            packed[place[i, j]:place[i, j] + TILE, :] = here[:, (j - i) * TILE:(j - i + 1) * TILE]
        block = here[:, :TILE]
        if i % 2:
            packed[place[i, i]:place[i, i] + TILE, :] = jnp.where(upper, even, block)
        even = block
        diagonals.append(jnp.sum(jnp.where(eye, block, 0.0), axis=0, keepdims=True))
    for copy in copies:
        copy.wait()
    values = held[...]
    present = seen[...].astype(jnp.float32)
    masked = present * values
    high, middle, low = (part.astype(jnp.float32) for part in split_three(masked))
    ones = jnp.ones(present.shape, jnp.float32)
    extra = jnp.concatenate([high, middle, low, present, ones, ones], 0).astype(jnp.bfloat16)
    products = dot_bf16(extra, padded[...], NT)
    sums = [jnp.sum(v, axis=1, keepdims=True) for v in (present, masked, masked * values)]
    for i in range(tiles):
        cols = slice(i * TILE, (i + 1) * TILE)
        row = side + SIDE * i
        total = products[0:8, cols] + products[8:16, cols] + products[16:24, cols]
        if i == tiles - 1:
            for n, value in enumerate(sums):
                total = jnp.where(lane == TILE - 1 - n, value, total)
        packed[row:row + 8, :] = total
        packed[row + 8:row + 16, :] = products[24:32, cols]
        packed[row + 16:row + 24, :] = jnp.where(line == 0, products[32:40, cols], diagonals[i])


def eliminate(work, old, count):
    fits = work.shape[0]
    shape = (fits, STEP, TILE)
    row, lane = iota(shape, 1), iota(shape, 2)
    per = SUB // STEP
    for t in range(count):
        base = t * STEP
        panel = work[:, base:base + STEP, :]
        cols = [
            jnp.broadcast_to(panel[:, :, base + m:base + m + 1], shape) for m in range(STEP)
        ]
        inside = jnp.logical_and(lane >= base, lane < base + STEP)
        panel = jnp.where(inside, jnp.where(lane - base == row, 1.0, 0.0), panel)
        old[:, base:base + STEP, :] = panel
        scale = None
        for j in range(STEP):
            inverse = jnp.broadcast_to(1.0 / cols[j][:, j:j + 1, :], shape)
            here = row == j
            gain = jnp.where(here, 0.0, cols[j] * inverse)
            scale = inverse if scale is None else jnp.where(here, inverse, scale)
            for m in range(j + 1, STEP):
                cols[m] = cols[m] - gain * cols[m][:, j:j + 1, :]
            panel = panel - gain * panel[:, j:j + 1, :]
        panel = panel * scale
        work[:, base:base + STEP, :] = panel
        rows = [jnp.broadcast_to(panel[:, q:q + 1, :], shape) for q in range(STEP)]
        stop = min((t // per + 1) * per, count)
        for g in range(t + 1, stop):
            other = work[:, g * STEP:(g + 1) * STEP, :]
            total = jnp.where(inside, 0.0, other)
            for q in range(STEP):
                total = total - jnp.broadcast_to(
                    other[:, :, base + q:base + q + 1], shape
                ) * rows[q]
            work[:, g * STEP:(g + 1) * STEP, :] = total
        if t + 1 == stop and stop < count:
            first, last = (t + 1 - per) * STEP, stop * STEP
            line, column = iota((SUB, TILE), 0) + first, iota((SUB, TILE), 1)
            keep = jnp.logical_or(column >= last, column // STEP <= line // STEP)
            column = iota((TILE - last, TILE), 1)
            done = jnp.logical_and(column >= first, column < last)
            for f in range(fits):
                left = split_three(old[f, first:last, :])
                right = split_three(jnp.where(keep, work[f, first:last, :], 0.0))
                product = dot_bf16(
                    jnp.concatenate([left[i] for i in (0, 0, 0, 1, 1, 2)], 0),
                    jnp.concatenate([right[i] for i in (0, 1, 2, 0, 1, 0)], 0),
                    TN,
                )
                rest = work[f, last:, :]
                work[f, last:, :] = jnp.where(done, 0.0, rest) - product[last:, :]


def fit_kernel(samples, markers, penalty, packed, out, stats, centre, grid, wide, work, old):
    fits = work.shape[0]
    tiles = out.shape[-1] // TILE
    end = tiles * TILE
    place, side = block_rows(tiles)

    def part(tile, which):
        row = side + SIDE * tile + 8 * which
        return packed[row:row + 8, :]

    sums = part(tiles - 1, 0)
    counts, first, second = (sums[:, TILE - 1 - n:TILE - n] for n in range(3))
    mean = first / counts
    spread = jnp.sqrt(second / counts - mean * mean + 1e-05)
    lane = iota((TRAITS, TILE), 1)
    stats[...] = jnp.where(lane == 0, mean, jnp.where(lane == 1, spread, 0.0))
    row, col = iota((TILE, TILE), 0), iota((TILE, TILE), 1)
    eye, upper = row == col, row <= col
    line = iota((1, TILE), 1)
    share = 1.0 / samples
    totals = [part(i, 2)[0:1, :] for i in range(tiles)]
    squares = []
    blank = jnp.zeros((TILE - TRAITS, TILE), jnp.float32)
    for i in range(tiles):
        mine = slice(i * TILE, (i + 1) * TILE)
        column = jnp.transpose(jnp.broadcast_to(totals[i], (TILE, TILE)))
        diagonal = part(i, 2)[1:2, :]
        middle = totals[i] * share
        centre[:, mine] = jnp.broadcast_to(middle, (8, TILE))
        squares.append(diagonal * share - middle * middle + 1e-05)
        for j in range(i, tiles):
            block = packed[place[i, j]:place[i, j] + TILE, :]
            if i == j:
                turned = jnp.transpose(block)
                if i % 2:
                    block = jnp.where(upper, turned, block)
                    block = jnp.where(eye, diagonal, block)
                else:
                    block = jnp.where(upper, block, turned)
            block = block - column * totals[j] * share
            if j == tiles - 1:
                value = (part(i, 0) - part(i, 1) * mean) / spread
                value = jnp.where(lane + i * TILE < markers, value, 0.0)
                block = block + jnp.transpose(jnp.concatenate([blank, value], 0))
            grid[i, :, j * TILE:(j + 1) * TILE] = block

    def ridge(i, f):
        value = jnp.where(line + i * TILE < markers, penalty[f] * squares[i], 1.0)
        return jnp.where(eye, value, 0.0)

    for f in range(fits):
        work[f] = grid[0, :, 0:TILE] + ridge(0, f)
    every = range(fits)
    count = TILE // STEP
    for k in range(tiles):
        lo, hi = k * TILE, (k + 1) * TILE
        pivots = count if hi < end else count - 1
        eliminate(work, old, pivots)
        lower = jnp.logical_and(col // STEP <= row // STEP, row < pivots * STEP)
        lefts = [jnp.where(lower, old[f], 0.0) for f in every]
        if hi < end:
            rights = [jnp.where(lower, work[f], 0.0) for f in every]
            above = [grid[0, :, hi:]] if k == 0 else [wide[f, k, :, hi:] for f in every]
            above = [right_parts(value) for value in above] * (fits if k == 0 else 1)
            stacked = [left_parts(jnp.concatenate([lefts[f], rights[f]], 0)) for f in every]
            both = products(stacked, above)
            factors = [left_parts(jnp.transpose(both[f][:TILE])) for f in every]
            parts = [right_parts(both[f][TILE:]) for f in every]
            for i in range(k + 1, tiles):
                begin = i * TILE
                after = products(
                    [[p[begin - hi:begin - hi + TILE] for p in factors[f]] for f in every],
                    [[p[:, begin - hi:] for p in parts[f]] for f in every],
                )
                for f in every:
                    before = grid[i, :, begin:] if k == 0 else wide[f, i, :, begin:]
                    value = before - after[f]
                    block = value[:, :TILE] + ridge(i, f) if k == 0 else value[:, :TILE]
                    if i == k + 1:
                        work[f] = block
                    else:
                        wide[f, i, :, begin:begin + TILE] = block
                    if i + 1 < tiles:
                        wide[f, i, :, begin + TILE:] = value[:, TILE:]
        else:
            last = jnp.logical_and(row < pivots * STEP, col >= pivots * STEP)
            parts = [right_parts(jnp.where(last, work[f], 0.0)) for f in every]
        final = products([left_parts(jnp.transpose(left)) for left in lefts], parts)
        for f in every:
            if hi < end:
                wide[f, k, :, hi:] = final[f]
            out[f, :, lo:hi] = jnp.transpose(final[f][:, -TILE:])[TILE - TRAITS:, :]
    for k in reversed(range(tiles - 1)):
        lo, hi = k * TILE, (k + 1) * TILE
        known = [dot(out[f, :, hi:], wide[f, k, :, hi:], NT) for f in every]
        for f in every:
            out[f, :, lo:hi] = out[f, :, lo:hi] - known[f]


def predict_kernel(pairs, place, mine, other, centre, padded, out):
    odd = place[0] == 1
    rows = []
    for f in range(HALF):
        rows.append(jnp.where(odd, other[f], mine[f]))
    for f in range(HALF):
        rows.append(jnp.where(odd, mine[f], other[f]))
    if pairs:
        upper = iota(rows[0].shape, 0) < TRAITS // 2
        second = place[1] == 1
        halves = [[], []]
        for s in range(0, SLOTS, 2):
            a, b = rows[s], rows[s + 1]
            turned_a, turned_b = (pltpu.roll(v, TRAITS // 2, 0) for v in (a, b))
            low, high = jnp.where(upper, a, turned_b), jnp.where(upper, turned_a, b)
            halves[0].append(jnp.where(second, high, low))
            halves[1].append(jnp.where(second, low, high))
        rows = halves[0] + halves[1]
    weights = jnp.concatenate(rows, 0)
    count = weights.shape[0]
    shift = jnp.sum(weights * centre[0:1, :], axis=1, keepdims=True)
    parts = [part.astype(jnp.float32) for part in split_three(weights)]
    product = dot_bf16(jnp.concatenate(parts, 0).astype(jnp.bfloat16), padded[...])
    total = product[0:count] + product[count:2 * count] + product[2 * count:3 * count] - shift
    if pairs:
        out[0] = total[:count // 2]
        out[1] = total[count // 2:]
    else:
        out[...] = total


def stack_kernel(pairs, per_share, place, mine, other, stats, traits, observed, folds, out):
    first = place[1] * per_share
    if pairs:
        second = place[1] == 1
        levels = jnp.concatenate(
            [jnp.where(second, other[...], mine[...]), jnp.where(second, mine[...], other[...])], 0
        )
    else:
        levels = mine[...]
    count, samples = levels.shape
    height, width = out.shape
    present = observed[...].astype(jnp.float32)
    scaled = present * (traits[...] - stats[:, 0:1]) / stats[:, 1:2]
    pick = iota((count, TRAITS), 1) == first + iota((count, TRAITS), 0) % per_share
    spread = dot_bf16(
        jnp.where(pick, 1.0, 0.0).astype(jnp.bfloat16), present.astype(jnp.bfloat16)
    )
    masks = [
        (spread * jnp.where(folds[...] == k, 1.0, 0.0)).astype(jnp.bfloat16) for k in range(FOLDS)
    ]
    right = split_three(jnp.concatenate([levels, scaled], 0))[:2]
    none = jnp.zeros((width - FOLDS * count, samples), jnp.bfloat16)
    left = [
        jnp.concatenate([part * mask for mask in masks] + [none], 0)
        for part in split_three(levels)[:2]
    ]
    full = dot_bf16(right[1], left[0], NT) + dot_bf16(
        jnp.concatenate([right[0], right[0]], 1), jnp.concatenate([left[1], left[0]], 1), NT
    )
    row, col = iota(full.shape, 0), iota(full.shape, 1)
    trait = jnp.where(row < count, row % per_share, row - count - first)
    full = jnp.where(trait == col % per_share, full, 0.0)
    shape = (height, full.shape[0])
    level, source = iota(shape, 0), iota(shape, 1)
    slot = source // per_share
    group = jnp.where(slot % SLOTS < FITS, slot // SLOTS * FITS + slot % SLOTS, height)
    group = jnp.where(source < count, group, count // per_share // SLOTS * FITS)
    out[...] = dot(jnp.where(level == group, 1.0, 0.0), full)
    ones = jnp.ones((16, samples), jnp.bfloat16)
    squares = split_three(levels * levels)
    energy = dot_bf16(ones, squares[1], NT) + dot_bf16(ones, squares[0], NT)
    last = count // per_share // SLOTS * FITS + 1
    out[last:last + 1, 0:count] = energy[0:1, :]


def scale_kernel(per_share, blocks, samples, total, gram, cross):
    height, width = total.shape
    count = blocks * SLOTS * per_share
    levels = blocks * FITS
    value = total[...]
    energy = jnp.broadcast_to(value[levels + 1:levels + 2, 0:count], (height, count))
    level, column = iota((height, count), 0), iota((height, count), 1) // per_share
    group = jnp.where(column % SLOTS < FITS, column // SLOTS * FITS + column % SLOTS, height)
    shape = (count, width)
    source, target = iota(shape, 0), iota(shape, 1)
    by_row = dot(
        jnp.where(level == group, energy, 0.0),
        jnp.where(source % per_share == target % per_share, 1.0, 0.0),
    )
    by_column = dot(energy, jnp.where(source == target % count, 1.0, 0.0))
    root_row = jnp.where(
        iota((height, width), 0) < levels, jnp.sqrt(by_row / samples + 1e-06), 1.0
    )
    root_column = jnp.sqrt(by_column / samples + 1e-06)
    value = value / root_row / root_column * (FOLDS / samples)
    turned = jnp.transpose(value)
    shape = (FOLDS * 8, width)
    line, column = iota(shape, 0), iota(shape, 1)
    chosen = jnp.logical_and(line // 8 == column // count, line % 8 == column % per_share)
    products = jnp.where(chosen, jnp.broadcast_to(value[levels:levels + 1, :], shape), 0.0)
    shape = (width, TILE)
    slot, target = iota(shape, 0) % count // per_share, iota(shape, 1)
    group = jnp.where(slot % SLOTS < FITS, slot // SLOTS * FITS + slot % SLOTS, -1)
    products = dot(products, jnp.where(group == target, 1.0, 0.0))
    for k in range(FOLDS):
        cross[k] = products[8 * k:8 * k + per_share, 0:levels]
        for l in range(levels):
            row = k * count + (l // FITS * SLOTS + l % FITS) * per_share
            gram[k, l] = turned[row:row + per_share, 0:levels]


def fit_scratch(fits, tiles, width):
    shapes = [(tiles, TILE, width), (fits, tiles, TILE, width)] + [(fits, TILE, TILE)] * 2
    return [pltpu.VMEM(shape, jnp.float32) for shape in shapes]


def swap(value, axis, mask):
    size = lax.axis_size(axis)
    return lax.ppermute(value, axis, [(i, i ^ mask) for i in range(size)])


def masks_of(axis):
    size, mask, found = lax.axis_size(axis), 1, []
    while mask < size:
        found.append(mask)
        mask *= 2
    return found


def sum_over(value, axis, halvings):
    masks = masks_of(axis)
    position = lax.axis_index(axis)
    for mask in masks[:halvings]:
        half = value.shape[0] // 2
        low, high = value[:half], value[half:]
        up = (position & mask) != 0
        value = jnp.where(up, high, low) + swap(jnp.where(up, low, high), axis, mask)
    for mask in masks[halvings:]:
        value = value + swap(value, axis, mask)
    for mask in reversed(masks[:halvings]):
        up = (position & mask) != 0
        other = swap(value, axis, mask)
        value = jnp.concatenate([jnp.where(up, other, value), jnp.where(up, value, other)], 0)
    return value


def body(genotypes, traits, observed, fold_index):
    local_rows, markers = genotypes.shape
    sample_devices = lax.axis_size("samp")
    block_devices = lax.axis_size("blk")
    samples = local_rows * sample_devices
    all_markers = markers * block_devices
    width = -(-markers // TILE) * TILE
    tiles = width // TILE
    per_share = TRAITS // block_devices
    pairs = block_devices == 2
    f32 = functools.partial(jax.ShapeDtypeStruct, dtype=jnp.float32)
    position, block = lax.axis_index("samp"), lax.axis_index("blk")
    odd = position % 2
    place = jnp.stack([odd, block]).astype(jnp.int32)
    traits, observed = traits.T, observed.T
    _, side = block_rows(tiles)

    whole = lambda shape: pl.BlockSpec(shape, lambda _: (0, 0))
    packed, padded = pl.pallas_call(
        functools.partial(gram_kernel, markers),
        grid=(1,),
        out_shape=[
            f32((side + SIDE * tiles, TILE)),
            jax.ShapeDtypeStruct((width, local_rows), jnp.bfloat16),
        ],
        in_specs=[whole((width, local_rows))] + [pl.BlockSpec(memory_space=pltpu.HBM)] * 2,
        out_specs=[whole((side + SIDE * tiles, TILE)), whole((width, local_rows))],
        scratch_shapes=[
            pltpu.VMEM(traits.shape, traits.dtype),
            pltpu.VMEM(observed.shape, observed.dtype),
            pltpu.SemaphoreType.DMA((2,)),
        ],
        compiler_params=pltpu.CompilerParams(vmem_limit_bytes=VMEM_BYTES),
        name="local_gram",
    )(genotypes.T, traits, observed)
    packed = sum_over(packed, "samp", 2)

    penalties = [all_markers * (1.0 - h) / h for h in HERITABILITY]
    penalties = penalties + [penalties[-1]] * (SLOTS - len(penalties))
    penalty = jnp.where(
        odd == 1,
        jnp.array(penalties[HALF:], jnp.float32),
        jnp.array(penalties[:HALF], jnp.float32),
    )
    weights, stats, centre = call(
        functools.partial(fit_kernel, samples, markers),
        [f32((HALF, TRAITS, width)), f32((TRAITS, TILE)), f32((8, width))],
        ["smem", "vmem"],
        fit_scratch(HALF, tiles, width),
        "ridge_fits",
    )(penalty, packed)
    other = swap(weights, "samp", 1)

    count = SLOTS * TRAITS
    shape = (2, count // 2, local_rows) if pairs else (count, local_rows)
    predicted = call(
        functools.partial(predict_kernel, pairs),
        f32(shape),
        ["smem", "vmem", "vmem", "vmem", "vmem"],
        [],
        "predictions",
    )(place, weights, other, centre, padded)
    if pairs:
        mine, theirs = predicted[0], swap(predicted[1], "blk", 1)
    else:
        shares = predicted.reshape(SLOTS, block_devices, per_share, local_rows)
        shares = lax.all_to_all(shares, "blk", split_axis=1, concat_axis=0, tiled=True)
        mine = theirs = shares.reshape(count, local_rows)

    levels = block_devices * FITS
    height = -(-(levels + 2) // 8) * 8
    lanes = -(-FOLDS * count // TILE) * TILE
    products = call(
        functools.partial(stack_kernel, pairs, per_share),
        f32((height, lanes)),
        ["smem"] + ["vmem"] * 6,
        [],
        "stacking",
    )(place, mine, theirs, stats, traits, observed, fold_index[None, :])
    products = sum_over(products, "samp", 0)
    gram, cross = call(
        functools.partial(scale_kernel, per_share, block_devices, samples),
        [f32((FOLDS, levels, per_share, levels)), f32((FOLDS, per_share, levels))],
        ["vmem"],
        [],
        "standardize",
    )(products)
    return gram.transpose(2, 0, 1, 3), cross.transpose(1, 0, 2)


def solution(mesh):
    in_specs = (P("samp", "blk"), P("samp", None), P("samp", None), P("samp"))
    out_specs = (P("blk", None, None, None), P("blk", None, None))
    return jax.shard_map(body, mesh=mesh, in_specs=in_specs, out_specs=out_specs, check_vma=False)
```

```python
import functools
import jax
import jax.numpy as jnp
from jax import lax
from jax.experimental import pallas as pl
from jax.experimental.pallas import tpu as pltpu
from jax.sharding import PartitionSpec as P

TRAITS = 8
FOLDS = 5
HERITABILITY = (0.01, 0.25, 0.5, 0.75, 0.99)
TILE = 128
STEP = 8
SIDE = 24
SUB = 32
TILES = 4
HALF_ROWS = 4 * TILE + 2 * SIDE
FITS = len(HERITABILITY)
SLOTS = 6
HALF = SLOTS // 2
VMEM_BYTES = 32 * 1024 * 1024

NN = (((1,), (0,)), ((), ()))
NT = (((1,), (1,)), ((), ()))
TN = (((0,), (0,)), ((), ()))


def dot(a, b, dims=NN):
    return lax.dot_general(
        a, b, dims, precision=lax.Precision.HIGHEST, preferred_element_type=jnp.float32
    )


def dot_bf16(a, b, dims=NN):
    return lax.dot_general(a, b, dims, preferred_element_type=jnp.float32)


def split_three(value):
    high = value.astype(jnp.bfloat16)
    left = value - high.astype(jnp.float32)
    middle = left.astype(jnp.bfloat16)
    low = (left - middle.astype(jnp.float32)).astype(jnp.bfloat16)
    return high, middle, low


def iota(shape, dim):
    return lax.broadcasted_iota(jnp.int32, shape, dim)


def left_parts(value):
    high, middle, low = split_three(value)
    return [jnp.concatenate(pair, 1) for pair in ((low, middle), (middle, high), (high, high))]


def right_parts(value):
    high, middle, low = split_three(value)
    first = jnp.concatenate([high, middle], 0)
    return [first, first, jnp.concatenate([low, high], 0)]


def products(lefts, rights):
    totals = [dot_bf16(a[0], b[0]) for a, b in zip(lefts, rights)]
    for part in (1, 2):
        terms = [dot_bf16(a[part], b[part]) for a, b in zip(lefts, rights)]
        totals = [total + term for total, term in zip(totals, terms)]
    return totals


def half_rows(part):
    return {"square": 0, "between": TILE, "cross": 2 * TILE, "side": 4 * TILE}[part]


def call(kernel, out_shape, in_specs, scratch, name, cost=None):
    vmem = pl.BlockSpec(memory_space=pltpu.VMEM)
    smem = pl.BlockSpec(memory_space=pltpu.SMEM)
    return pl.pallas_call(
        kernel,
        out_shape=out_shape,
        in_specs=[smem if spec == "smem" else vmem for spec in in_specs],
        out_specs=jax.tree.map(lambda _: vmem, out_shape),
        scratch_shapes=scratch,
        compiler_params=pltpu.CompilerParams(vmem_limit_bytes=VMEM_BYTES),
        cost_estimate=cost,
        name=name,
    )


def gram_kernel(markers, dosage, traits, observed, packed, padded, held, seen, arrived):
    copies = [
        pltpu.make_async_copy(traits, held, arrived.at[0]),
        pltpu.make_async_copy(observed, seen, arrived.at[1]),
    ]
    for copy in copies:
        copy.start()
    width, rows = padded.shape
    tiles = width // TILE
    edge = markers // 16 * 16
    padded[0:edge, :] = dosage[0:edge, :]
    tail = dosage[edge:edge + 16, :].astype(jnp.float32)
    tail = jnp.where(iota(tail.shape, 0) + edge < markers, tail, 0.0)
    padded[edge:edge + 16, :] = tail.astype(jnp.bfloat16)
    if edge + 16 < width:
        padded[edge + 16:, :] = jnp.zeros((width - edge - 16, rows), jnp.bfloat16)
    lane, line = iota((TRAITS, TILE), 1), iota((TRAITS, TILE), 0)
    upper = iota((TILE, TILE), 0) <= iota((TILE, TILE), 1)
    eye = iota((TILE, TILE), 0) == iota((TILE, TILE), 1)
    even, diagonals = None, []
    for i in range(tiles):
        here = dot_bf16(padded[i * TILE:(i + 1) * TILE, :], padded[i * TILE:, :], NT)
        top = i // 2 * HALF_ROWS
        for j in range(i + 1, tiles):
            if j // 2 == i // 2:
                row = top + half_rows("between")
            else:
                row = i * HALF_ROWS + half_rows("cross") + j % 2 * TILE
            packed[row:row + TILE, :] = here[:, (j - i) * TILE:(j - i + 1) * TILE]
        block = here[:, :TILE]
        if i % 2:
            row = top + half_rows("square")
            packed[row:row + TILE, :] = jnp.where(upper, even, block)
        even = block
        diagonals.append(jnp.sum(jnp.where(eye, block, 0.0), axis=0, keepdims=True))
    for copy in copies:
        copy.wait()
    values = held[...]
    present = seen[...].astype(jnp.float32)
    masked = present * values
    high, middle, low = (part.astype(jnp.float32) for part in split_three(masked))
    ones = jnp.ones(present.shape, jnp.float32)
    extra = jnp.concatenate([high, middle, low, present, ones, ones], 0).astype(jnp.bfloat16)
    products = dot_bf16(extra, padded[...], NT)
    sums = [jnp.sum(v, axis=1, keepdims=True) for v in (present, masked, masked * values)]
    for i in range(tiles):
        cols = slice(i * TILE, (i + 1) * TILE)
        row = i // 2 * HALF_ROWS + half_rows("side") + i % 2 * SIDE
        total = products[0:8, cols] + products[8:16, cols] + products[16:24, cols]
        if i == tiles - 1:
            for n, value in enumerate(sums):
                total = jnp.where(lane == TILE - 1 - n, value, total)
        packed[row:row + 8, :] = total
        packed[row + 8:row + 16, :] = products[24:32, cols]
        packed[row + 16:row + 24, :] = jnp.where(line == 0, products[32:40, cols], diagonals[i])


def own(ref, fit, first=0, last=TILE):
    return ref.at[fit * TILE + first:fit * TILE + last, :]


def eliminate(work, old, fits):
    count, per, every = TILE // STEP, SUB // STEP, range(fits)
    lane, lane_step = iota((fits, TILE), 1), iota((STEP, TILE), 1)
    shape = (STEP, TILE)
    for t in range(count):
        base = t * STEP
        rows = [work[pl.ds(base + i, fits, stride=TILE), :] for i in range(STEP)]
        cells = [
            [jnp.broadcast_to(rows[i][:, base + j:base + j + 1], rows[i].shape) for j in range(i + 1)]
            for i in range(STEP)
        ]
        inside = jnp.logical_and(lane >= base, lane < base + STEP)
        for i in range(STEP):
            rows[i] = jnp.where(inside, jnp.where(lane == base + i, 1.0, 0.0), rows[i])
            old[pl.ds(base + i, fits, stride=TILE), :] = rows[i]
        gains, inverses = {}, []
        for j in range(STEP):
            inverses.append(1.0 / cells[j][j])
            for i in range(j + 1, STEP):
                gains[i, j] = cells[i][j] * inverses[j]
            for i in range(j + 1, STEP):
                for m in range(j + 1, i + 1):
                    cells[i][m] = cells[i][m] - gains[i, j] * cells[m][j]
            for i in range(j + 1, STEP):
                rows[i] = rows[i] - gains[i, j] * rows[j]
        rows = [value * inverse for value, inverse in zip(rows, inverses)]
        for j in reversed(range(1, STEP)):
            for i in range(j):
                rows[i] = rows[i] - gains[j, i] * rows[j]
        for i in range(STEP):
            work[pl.ds(base + i, fits, stride=TILE), :] = rows[i]
        stop = (t // per + 1) * per
        if t + 1 < stop:
            spread = [
                [
                    jnp.broadcast_to(own(work, f, base + q, base + q + 1)[...], shape)
                    for f in every
                ]
                for q in range(STEP)
            ]
            inside = jnp.logical_and(lane_step >= base, lane_step < base + STEP)
            for g in range(t + 1, stop):
                refs = [own(work, f, g * STEP, (g + 1) * STEP) for f in every]
                others = [ref[...] for ref in refs]
                totals = [jnp.where(inside, 0.0, other) for other in others]
                for q in range(STEP):
                    for f in every:
                        factor = jnp.broadcast_to(others[f][:, base + q:base + q + 1], shape)
                        totals[f] = totals[f] - factor * spread[q][f]
                for f in every:
                    refs[f][...] = totals[f]
        elif stop < count:
            first, last = (t + 1 - per) * STEP, stop * STEP
            line, column = iota((SUB, TILE), 0) + first, iota((SUB, TILE), 1)
            keep = jnp.logical_or(column >= last, column // STEP <= line // STEP)
            column = iota((TILE - last, TILE), 1)
            done = jnp.logical_and(column >= first, column < last)
            lefts, rights = [], []
            for f in every:
                left = split_three(own(old, f, first, last)[...])
                right = split_three(jnp.where(keep, own(work, f, first, last)[...], 0.0))
                lefts.append(jnp.concatenate([left[i] for i in (0, 0, 0, 1, 1, 2)], 0))
                rights.append(jnp.concatenate([right[i] for i in (0, 1, 2, 0, 1, 0)], 0))
            terms = [dot_bf16(a, b, TN) for a, b in zip(lefts, rights)]
            for f in every:
                rest = own(work, f, last)
                rest[...] = jnp.where(done, 0.0, rest[...]) - terms[f][last:, :]


class Half:
    def __init__(self, ref, first, samples, markers):
        row, col = iota((TILE, TILE), 0), iota((TILE, TILE), 1)
        self.eye, self.ref, self.share = row == col, ref, 1.0 / samples
        self.totals, self.squares, self.valid = [], [], []
        for tile in range(2):
            start = half_rows("side") + SIDE * tile + 16
            total, diagonal = ref[start:start + 1, :], ref[start + 1:start + 2, :]
            middle = total * self.share
            self.totals.append(total)
            self.squares.append(diagonal * self.share - middle * middle + 1e-05)
            self.valid.append(iota((1, TILE), 1) + (first + tile) * TILE < markers)
        self.columns = [jnp.transpose(jnp.broadcast_to(t, (TILE, TILE))) for t in self.totals]

    def block(self, part, index=0):
        row = half_rows(part) + index * TILE
        return self.ref[row:row + TILE, :]

    def centred(self):
        square = self.block("square")
        turned = jnp.transpose(square)
        upper = iota((TILE, TILE), 0) <= iota((TILE, TILE), 1)
        start = half_rows("side") + SIDE + 16
        second = jnp.where(upper, turned, square)
        second = jnp.where(self.eye, self.ref[start + 1:start + 2, :], second)
        blocks = [jnp.where(upper, square, turned), self.block("between"), second]
        pairs = [(0, 0), (0, 1), (1, 1)]
        return [
            block - self.columns[i] * self.totals[j] * self.share
            for block, (i, j) in zip(blocks, pairs)
        ]

    def ridge(self, tile, penalty):
        value = jnp.where(self.valid[tile], penalty * self.squares[tile], 1.0)
        return jnp.where(self.eye, value, 0.0)

    def side(self, tile, which):
        start = half_rows("side") + SIDE * tile + 8 * which
        return self.ref[start:start + 8, :]


def lower_part(value):
    keep = iota((TILE, TILE), 1) // STEP <= iota((TILE, TILE), 0) // STEP
    return jnp.where(keep, value, 0.0)


def first_kernel(samples, markers, penalty, place, mine, lefts, rights, above, weights, work, old):
    fits = lefts.shape[0]
    every = range(fits)
    half = Half(mine, 2 * place[2], samples, markers)
    first, between, second = half.centred()
    for f in every:
        own(work, f)[...] = first + half.ridge(0, penalty[f])
    eliminate(work, old, fits)
    for f in every:
        lefts[f, 0], rights[f, 0] = lower_part(own(old, f)[...]), lower_part(own(work, f)[...])
    parts = right_parts(between)
    both = products(
        [left_parts(jnp.concatenate([lefts[f, 0], rights[f, 0]], 0)) for f in every],
        [parts for f in every],
    )
    after = products(
        [left_parts(jnp.transpose(both[f][:TILE])) for f in every],
        [right_parts(both[f][TILE:]) for f in every],
    )
    for f in every:
        above[f], weights[f] = both[f][:TILE], both[f][TILE:]
        own(work, f)[...] = second - after[f] + half.ridge(1, penalty[f])
    eliminate(work, old, fits)
    for f in every:
        lefts[f, 1], rights[f, 1] = lower_part(own(old, f)[...]), lower_part(own(work, f)[...])


def second_kernel(
    samples, markers, penalty, place, mine, theirs, lefts, rights, above, weights,
    out, stats, centre, wide, work, old, rhs, scratch,
):
    fits = out.shape[0]
    every = range(fits)
    late = place[2] == 1
    halves = [Half(mine, 2 * place[2], samples, markers)]
    halves.append(Half(theirs, 2 - 2 * place[2], samples, markers))
    sums = jnp.where(late, halves[0].side(1, 0), halves[1].side(1, 0))
    counts, first, second = (sums[:, TILE - 1 - n:TILE - n] for n in range(3))
    mean = first / counts
    spread = jnp.sqrt(second / counts - mean * mean + 1e-05)
    lane = iota((TRAITS, TILE), 1)
    stats[...] = jnp.where(lane == 0, mean, jnp.where(lane == 1, spread, 0.0))
    share = 1.0 / samples

    def place_tiles(ref, index, tiles):
        for t in range(TILES):
            value = jnp.where(late, tiles[(t + 2) % TILES], tiles[t])
            cols = slice(t * TILE, (t + 1) * TILE)
            if index is None:
                ref[:, cols] = value
            else:
                ref[index, :, cols] = value

    tiles = [(halves[t // 2], t % 2) for t in range(TILES)]
    totals = [half.totals[t] for half, t in tiles]
    place_tiles(centre, None, [jnp.broadcast_to(t * share, (8, TILE)) for t in totals])
    for t, (half, tile) in enumerate(tiles):
        value = (half.side(tile, 0) - half.side(tile, 1) * mean) / spread
        value = jnp.where(half.valid[tile], value, 0.0)
        for f in every:
            rhs[f, :, t * TILE:(t + 1) * TILE] = value
    a, b = (halves[0].block("cross", n) for n in range(2))
    c, d = (halves[1].block("cross", n) for n in range(2))
    crosses = [
        [jnp.where(late, c.T, a), jnp.where(late, a.T, b)],
        [jnp.where(late, d.T, c), jnp.where(late, b.T, d)],
    ]
    rows = []
    for i in range(2):
        column = halves[0].columns[i]
        rows.append(
            jnp.concatenate(
                [crosses[i][j] - column * totals[2 + j] * share for j in range(2)], 1
            )
        )
    blocks = halves[1].centred()
    corner = [jnp.concatenate(blocks[:2], 1), blocks[2]]
    ridge = [[halves[1].ridge(t, penalty[f]) for t in range(2)] for f in every]

    def stacked(k):
        return [left_parts(jnp.concatenate([lefts[f, k], rights[f, k]], 0)) for f in every]

    def side_step(k, left, right, later):
        lo, hi = k * TILE, (k + 1) * TILE
        turned = [dot(rhs[f, :, lo:hi], left[f], NT) for f in every]
        for f in every:
            rhs[f, :, lo:hi] = dot(turned[f], right[f])
            if later is not None:
                rhs[f, :, hi:] = rhs[f, :, hi:] - dot(turned[f], later[f])

    parts = right_parts(rows[0])
    both = products(stacked(0), [parts for f in every])
    after = products(
        [left_parts(jnp.transpose(above[f])) for f in every],
        [right_parts(both[f][TILE:]) for f in every],
    )
    parts = [right_parts(rows[1] - after[f]) for f in every]
    more = products(stacked(1), parts)
    upper = [jnp.concatenate([both[f][:TILE], more[f][:TILE]], 0) for f in every]
    lower = [jnp.concatenate([both[f][TILE:], more[f][TILE:]], 0) for f in every]
    factors = [left_parts(jnp.transpose(upper[f])) for f in every]
    parts = [right_parts(lower[f]) for f in every]
    for i in range(2):
        cut = i * TILE
        after = products(
            [[p[cut:cut + TILE] for p in factors[f]] for f in every],
            [[p[:, cut:] for p in parts[f]] for f in every],
        )
        for f in every:
            value = corner[i] - after[f]
            block = value[:, :TILE] + ridge[f][i]
            if i == 0:
                own(work, f)[...] = block
                scratch[f, 0] = value[:, TILE:]
            else:
                scratch[f, 1] = block
    later = [jnp.concatenate([weights[f], both[f][TILE:]], 1) for f in every]
    side_step(0, [lefts[f, 0] for f in every], [rights[f, 0] for f in every], later)
    final = products(
        [left_parts(jnp.transpose(lefts[f, 0])) for f in every], [right_parts(v) for v in later]
    )
    for f in every:
        wide[f, 0, :, TILE:] = final[f]
    later = [more[f][TILE:] for f in every]
    side_step(1, [lefts[f, 1] for f in every], [rights[f, 1] for f in every], later)
    final = products(
        [left_parts(jnp.transpose(lefts[f, 1])) for f in every], [right_parts(v) for v in later]
    )
    for f in every:
        wide[f, 1, :, 2 * TILE:] = final[f]

    eliminate(work, old, fits)
    left = [lower_part(own(old, f)[...]) for f in every]
    right = [lower_part(own(work, f)[...]) for f in every]
    both = products(
        [left_parts(jnp.concatenate([left[f], right[f]], 0)) for f in every],
        [right_parts(scratch[f, 0]) for f in every],
    )
    later = [both[f][TILE:] for f in every]
    parts = [right_parts(v) for v in later]
    after = products([left_parts(jnp.transpose(both[f][:TILE])) for f in every], parts)
    for f in every:
        own(work, f)[...] = scratch[f, 1] - after[f]
    side_step(2, left, right, later)
    final = products([left_parts(jnp.transpose(left[f])) for f in every], parts)
    for f in every:
        wide[f, 2, :, 3 * TILE:] = final[f]
    eliminate(work, old, fits)
    left = [lower_part(own(old, f)[...]) for f in every]
    right = [lower_part(own(work, f)[...]) for f in every]
    side_step(3, left, right, None)
    for k in reversed(range(TILES - 1)):
        lo, hi = k * TILE, (k + 1) * TILE
        known = [dot(rhs[f, :, hi:], wide[f, k, :, hi:], NT) for f in every]
        for f in every:
            rhs[f, :, lo:hi] = rhs[f, :, lo:hi] - known[f]
    for f in every:
        place_tiles(out, f, [rhs[f, :, t * TILE:(t + 1) * TILE] for t in range(TILES)])


def predict_kernel(pairs, place, mine, other, centre, padded, out):
    odd = place[0] == 1
    rows = []
    for f in range(HALF):
        rows.append(jnp.where(odd, other[f], mine[f]))
    for f in range(HALF):
        rows.append(jnp.where(odd, mine[f], other[f]))
    if pairs:
        upper = iota(rows[0].shape, 0) < TRAITS // 2
        second = place[1] == 1
        halves = [[], []]
        for s in range(0, SLOTS, 2):
            a, b = rows[s], rows[s + 1]
            turned_a, turned_b = (pltpu.roll(v, TRAITS // 2, 0) for v in (a, b))
            low, high = jnp.where(upper, a, turned_b), jnp.where(upper, turned_a, b)
            halves[0].append(jnp.where(second, high, low))
            halves[1].append(jnp.where(second, low, high))
        rows = halves[0] + halves[1]
    weights = jnp.concatenate(rows, 0)
    count = weights.shape[0]
    shift = jnp.sum(weights * centre[0:1, :], axis=1, keepdims=True)
    parts = [part.astype(jnp.float32) for part in split_three(weights)]
    product = dot_bf16(jnp.concatenate(parts, 0).astype(jnp.bfloat16), padded[...])
    total = product[0:count] + product[count:2 * count] + product[2 * count:3 * count] - shift
    if pairs:
        out[0] = total[:count // 2]
        out[1] = total[count // 2:]
    else:
        out[...] = total


def stack_kernel(pairs, per_share, place, mine, other, stats, traits, observed, folds, out):
    first = place[1] * per_share
    if pairs:
        second = place[1] == 1
        levels = jnp.concatenate(
            [jnp.where(second, other[...], mine[...]), jnp.where(second, mine[...], other[...])], 0
        )
    else:
        levels = mine[...]
    count, samples = levels.shape
    height, width = out.shape
    present = observed[...].astype(jnp.float32)
    scaled = present * (traits[...] - stats[:, 0:1]) / stats[:, 1:2]
    pick = iota((count, TRAITS), 1) == first + iota((count, TRAITS), 0) % per_share
    spread = dot_bf16(
        jnp.where(pick, 1.0, 0.0).astype(jnp.bfloat16), present.astype(jnp.bfloat16)
    )
    masks = [
        (spread * jnp.where(folds[...] == k, 1.0, 0.0)).astype(jnp.bfloat16) for k in range(FOLDS)
    ]
    right = split_three(jnp.concatenate([levels, scaled], 0))[:2]
    none = jnp.zeros((width - FOLDS * count, samples), jnp.bfloat16)
    left = [
        jnp.concatenate([part * mask for mask in masks] + [none], 0)
        for part in split_three(levels)[:2]
    ]
    full = dot_bf16(right[1], left[0], NT) + dot_bf16(
        jnp.concatenate([right[0], right[0]], 1), jnp.concatenate([left[1], left[0]], 1), NT
    )
    row, col = iota(full.shape, 0), iota(full.shape, 1)
    trait = jnp.where(row < count, row % per_share, row - count - first)
    full = jnp.where(trait == col % per_share, full, 0.0)
    shape = (height, full.shape[0])
    level, source = iota(shape, 0), iota(shape, 1)
    slot = source // per_share
    group = jnp.where(slot % SLOTS < FITS, slot // SLOTS * FITS + slot % SLOTS, height)
    group = jnp.where(source < count, group, count // per_share // SLOTS * FITS)
    out[...] = dot(jnp.where(level == group, 1.0, 0.0), full)
    ones = jnp.ones((16, samples), jnp.bfloat16)
    squares = split_three(levels * levels)
    energy = dot_bf16(ones, squares[1], NT) + dot_bf16(ones, squares[0], NT)
    last = count // per_share // SLOTS * FITS + 1
    out[last:last + 1, 0:count] = energy[0:1, :]


def scale_kernel(per_share, blocks, samples, total, gram, cross):
    height, width = total.shape
    count = blocks * SLOTS * per_share
    levels = blocks * FITS
    value = total[...]
    energy = jnp.broadcast_to(value[levels + 1:levels + 2, 0:count], (height, count))
    level, column = iota((height, count), 0), iota((height, count), 1) // per_share
    group = jnp.where(column % SLOTS < FITS, column // SLOTS * FITS + column % SLOTS, height)
    shape = (count, width)
    source, target = iota(shape, 0), iota(shape, 1)
    by_row = dot(
        jnp.where(level == group, energy, 0.0),
        jnp.where(source % per_share == target % per_share, 1.0, 0.0),
    )
    by_column = dot(energy, jnp.where(source == target % count, 1.0, 0.0))
    root_row = jnp.where(
        iota((height, width), 0) < levels, jnp.sqrt(by_row / samples + 1e-06), 1.0
    )
    root_column = jnp.sqrt(by_column / samples + 1e-06)
    value = value / root_row / root_column * (FOLDS / samples)
    turned = jnp.transpose(value)
    shape = (FOLDS * 8, width)
    line, column = iota(shape, 0), iota(shape, 1)
    chosen = jnp.logical_and(line // 8 == column // count, line % 8 == column % per_share)
    products = jnp.where(chosen, jnp.broadcast_to(value[levels:levels + 1, :], shape), 0.0)
    shape = (width, TILE)
    slot, target = iota(shape, 0) % count // per_share, iota(shape, 1)
    group = jnp.where(slot % SLOTS < FITS, slot // SLOTS * FITS + slot % SLOTS, -1)
    products = dot(products, jnp.where(group == target, 1.0, 0.0))
    for k in range(FOLDS):
        cross[k] = products[8 * k:8 * k + per_share, 0:levels]
        for l in range(levels):
            row = k * count + (l // FITS * SLOTS + l % FITS) * per_share
            gram[k, l] = turned[row:row + per_share, 0:levels]


def swap(value, axis, mask):
    size = lax.axis_size(axis)
    return lax.ppermute(value, axis, [(i, i ^ mask) for i in range(size)])


def masks_of(axis):
    size, mask, found = lax.axis_size(axis), 1, []
    while mask < size:
        found.append(mask)
        mask *= 2
    return found


def sum_over(value, axis):
    for mask in masks_of(axis):
        value = value + swap(value, axis, mask)
    return value


def body(genotypes, traits, observed, fold_index):
    local_rows, markers = genotypes.shape
    sample_devices = lax.axis_size("samp")
    block_devices = lax.axis_size("blk")
    samples = local_rows * sample_devices
    all_markers = markers * block_devices
    width = -(-markers // TILE) * TILE
    assert width == TILES * TILE and markers + 3 <= width
    per_share = TRAITS // block_devices
    pairs = block_devices == 2
    f32 = functools.partial(jax.ShapeDtypeStruct, dtype=jnp.float32)
    position, block = lax.axis_index("samp"), lax.axis_index("blk")
    odd = position % 2
    late = position // 2 % 2
    place = jnp.stack([odd, block, late]).astype(jnp.int32)
    traits, observed = traits.T, observed.T

    whole = lambda shape: pl.BlockSpec(shape, lambda _: (0, 0))
    packed, padded = pl.pallas_call(
        functools.partial(gram_kernel, markers),
        grid=(1,),
        out_shape=[
            f32((2 * HALF_ROWS, TILE)),
            jax.ShapeDtypeStruct((width, local_rows), jnp.bfloat16),
        ],
        in_specs=[whole((width, local_rows))] + [pl.BlockSpec(memory_space=pltpu.HBM)] * 2,
        out_specs=[whole((2 * HALF_ROWS, TILE)), whole((width, local_rows))],
        scratch_shapes=[
            pltpu.VMEM(traits.shape, traits.dtype),
            pltpu.VMEM(observed.shape, observed.dtype),
            pltpu.SemaphoreType.DMA((2,)),
        ],
        compiler_params=pltpu.CompilerParams(vmem_limit_bytes=VMEM_BYTES),
        name="local_gram",
    )(genotypes.T, traits, observed)
    quarters = packed.reshape(2, 2, HALF_ROWS // 2, TILE)
    up = odd == 1
    keep = jnp.where(up, quarters[:, 1], quarters[:, 0])
    value = keep + swap(jnp.where(up, quarters[:, 0], quarters[:, 1]), "samp", 1)
    keep = jnp.where(late == 1, value[1], value[0])
    value = keep + swap(jnp.where(late == 1, value[0], value[1]), "samp", 2)
    for mask in masks_of("samp")[2:]:
        value = value + swap(value, "samp", mask)
    other = swap(value, "samp", 1)
    half = jnp.concatenate([jnp.where(up, other, value), jnp.where(up, value, other)], 0)
    theirs = swap(half, "samp", 2)

    penalties = [all_markers * (1.0 - h) / h for h in HERITABILITY]
    penalties = penalties + [penalties[-1]] * (SLOTS - len(penalties))
    penalty = jnp.where(
        odd == 1,
        jnp.array(penalties[HALF:], jnp.float32),
        jnp.array(penalties[:HALF], jnp.float32),
    )
    square = (HALF, TILE, TILE)
    started = call(
        functools.partial(first_kernel, samples, markers),
        [f32((HALF, 2, TILE, TILE)), f32((HALF, 2, TILE, TILE)), f32(square), f32(square)],
        ["smem", "smem", "vmem"],
        [pltpu.VMEM((HALF * TILE, TILE), jnp.float32)] * 2,
        "first_fits",
        cost=pl.CostEstimate(flops=4 * 10**9, bytes_accessed=2**21, transcendentals=0),
    )(penalty, place, half)
    weights, stats, centre = call(
        functools.partial(second_kernel, samples, markers),
        [f32((HALF, TRAITS, width)), f32((TRAITS, TILE)), f32((8, width))],
        ["smem", "smem"] + ["vmem"] * 6,
        [
            pltpu.VMEM((HALF, TILES, TILE, width), jnp.float32),
            pltpu.VMEM((HALF * TILE, TILE), jnp.float32),
            pltpu.VMEM((HALF * TILE, TILE), jnp.float32),
            pltpu.VMEM((HALF, TRAITS, width), jnp.float32),
            pltpu.VMEM((HALF, 2, TILE, TILE), jnp.float32),
        ],
        "second_fits",
    )(penalty, place, half, theirs, *started)
    other = swap(weights, "samp", 1)

    count = SLOTS * TRAITS
    shape = (2, count // 2, local_rows) if pairs else (count, local_rows)
    predicted = call(
        functools.partial(predict_kernel, pairs),
        f32(shape),
        ["smem", "vmem", "vmem", "vmem", "vmem"],
        [],
        "predictions",
    )(place, weights, other, centre, padded)
    if pairs:
        mine, theirs = predicted[0], swap(predicted[1], "blk", 1)
    else:
        shares = predicted.reshape(SLOTS, block_devices, per_share, local_rows)
        shares = lax.all_to_all(shares, "blk", split_axis=1, concat_axis=0, tiled=True)
        mine = theirs = shares.reshape(count, local_rows)

    levels = block_devices * FITS
    height = -(-(levels + 2) // 8) * 8
    lanes = -(-FOLDS * count // TILE) * TILE
    products = call(
        functools.partial(stack_kernel, pairs, per_share),
        f32((height, lanes)),
        ["smem"] + ["vmem"] * 6,
        [],
        "stacking",
    )(place, mine, theirs, stats, traits, observed, fold_index[None, :])
    products = sum_over(products, "samp")
    gram, cross = call(
        functools.partial(scale_kernel, per_share, block_devices, samples),
        [f32((FOLDS, levels, per_share, levels)), f32((FOLDS, per_share, levels))],
        ["vmem"],
        [],
        "standardize",
    )(products)
    return gram.transpose(2, 0, 1, 3), cross.transpose(1, 0, 2)


def solution(mesh):
    in_specs = (P("samp", "blk"), P("samp", None), P("samp", None), P("samp"))
    out_specs = (P("blk", None, None, None), P("blk", None, None))
    return jax.shard_map(body, mesh=mesh, in_specs=in_specs, out_specs=out_specs, check_vma=False)
```

```python
import functools
import jax
import jax.numpy as jnp
from jax import lax
from jax.experimental import pallas as pl
from jax.experimental.pallas import tpu as pltpu
from jax.sharding import PartitionSpec as P

TRAITS = 8
FOLDS = 5
HERITABILITY = (0.01, 0.25, 0.5, 0.75, 0.99)
TILE = 128
STEP = 8
SIDE = 24
SUB = 32
TILES = 4
HALF_ROWS = 4 * TILE + 2 * SIDE
FITS = len(HERITABILITY)
SLOTS = 6
HALF = SLOTS // 2
VMEM_BYTES = 32 * 1024 * 1024

NN = (((1,), (0,)), ((), ()))
NT = (((1,), (1,)), ((), ()))
TN = (((0,), (0,)), ((), ()))


def dot(a, b, dims=NN):
    return lax.dot_general(
        a, b, dims, precision=lax.Precision.HIGHEST, preferred_element_type=jnp.float32
    )


def dot_bf16(a, b, dims=NN):
    return lax.dot_general(a, b, dims, preferred_element_type=jnp.float32)


def split_three(value):
    high = value.astype(jnp.bfloat16)
    left = value - high.astype(jnp.float32)
    middle = left.astype(jnp.bfloat16)
    low = (left - middle.astype(jnp.float32)).astype(jnp.bfloat16)
    return high, middle, low


def iota(shape, dim):
    return lax.broadcasted_iota(jnp.int32, shape, dim)


def left_parts(value):
    high, middle, low = split_three(value)
    return [jnp.concatenate(pair, 1) for pair in ((low, middle), (middle, high), (high, high))]


def right_parts(value):
    high, middle, low = split_three(value)
    first = jnp.concatenate([high, middle], 0)
    return [first, first, jnp.concatenate([low, high], 0)]


def products(lefts, rights):
    totals = [dot_bf16(a[0], b[0]) for a, b in zip(lefts, rights)]
    for part in (1, 2):
        terms = [dot_bf16(a[part], b[part]) for a, b in zip(lefts, rights)]
        totals = [total + term for total, term in zip(totals, terms)]
    return totals


def half_rows(part):
    return {"square": 0, "between": TILE, "cross": 2 * TILE, "side": 4 * TILE}[part]


def call(kernel, out_shape, in_specs, scratch, name, cost=None):
    vmem = pl.BlockSpec(memory_space=pltpu.VMEM)
    smem = pl.BlockSpec(memory_space=pltpu.SMEM)
    return pl.pallas_call(
        kernel,
        out_shape=out_shape,
        in_specs=[smem if spec == "smem" else vmem for spec in in_specs],
        out_specs=jax.tree.map(lambda _: vmem, out_shape),
        scratch_shapes=scratch,
        compiler_params=pltpu.CompilerParams(vmem_limit_bytes=VMEM_BYTES),
        cost_estimate=cost,
        name=name,
    )


def gram_kernel(markers, dosage, masked, present, packed, padded):
    width, rows = padded.shape
    tiles = width // TILE
    edge = markers // 16 * 16
    padded[0:edge, :] = dosage[0:edge, :]
    tail = dosage[edge:edge + 16, :].astype(jnp.float32)
    tail = jnp.where(iota(tail.shape, 0) + edge < markers, tail, 0.0)
    padded[edge:edge + 16, :] = tail.astype(jnp.bfloat16)
    if edge + 16 < width:
        padded[edge + 16:, :] = jnp.zeros((width - edge - 16, rows), jnp.bfloat16)
    lane, line = iota((TRAITS, TILE), 1), iota((TRAITS, TILE), 0)
    upper = iota((TILE, TILE), 0) <= iota((TILE, TILE), 1)
    eye = iota((TILE, TILE), 0) == iota((TILE, TILE), 1)
    even, diagonals = None, []
    for i in range(tiles):
        here = dot_bf16(padded[i * TILE:(i + 1) * TILE, :], padded[i * TILE:, :], NT)
        top = i // 2 * HALF_ROWS
        for j in range(i + 1, tiles):
            if j // 2 == i // 2:
                row = top + half_rows("between")
            else:
                row = i * HALF_ROWS + half_rows("cross") + j % 2 * TILE
            packed[row:row + TILE, :] = here[:, (j - i) * TILE:(j - i + 1) * TILE]
        block = here[:, :TILE]
        if i % 2:
            row = top + half_rows("square")
            packed[row:row + TILE, :] = jnp.where(upper, even, block)
        even = block
        diagonals.append(jnp.sum(jnp.where(eye, block, 0.0), axis=0, keepdims=True))
    masked, present = masked[...], present[...]
    high, middle, low = (part.astype(jnp.float32) for part in split_three(masked))
    ones = jnp.ones(present.shape, jnp.float32)
    extra = jnp.concatenate([high, middle, low, present, ones, ones], 0).astype(jnp.bfloat16)
    products = dot_bf16(extra, padded[...], NT)
    sums = [jnp.sum(v, axis=1, keepdims=True) for v in (present, masked, masked * masked)]
    for i in range(tiles):
        cols = slice(i * TILE, (i + 1) * TILE)
        row = i // 2 * HALF_ROWS + half_rows("side") + i % 2 * SIDE
        total = products[0:8, cols] + products[8:16, cols] + products[16:24, cols]
        if i == tiles - 1:
            for n, value in enumerate(sums):
                total = jnp.where(lane == TILE - 1 - n, value, total)
        packed[row:row + 8, :] = total
        packed[row + 8:row + 16, :] = products[24:32, cols]
        packed[row + 16:row + 24, :] = jnp.where(line == 0, products[32:40, cols], diagonals[i])


def own(ref, fit, first=0, last=TILE):
    return ref.at[fit * TILE + first:fit * TILE + last, :]


def eliminate(work, old, flat, turned, fits):
    per, every = SUB // STEP, range(fits)
    lane, lane_step, row_step = iota((fits, TILE), 1), iota((STEP, TILE), 1), iota((STEP, TILE), 0)
    shape = (STEP, TILE)

    def spread(value, column):
        return jnp.broadcast_to(value[:, column:column + 1], value.shape)

    for first in range(0, TILE, SUB):
        last = first + SUB
        groups = [
            [own(work, f, first + g * STEP, first + (g + 1) * STEP)[...] for f in every]
            for g in range(per)
        ]
        before = []
        for t in range(per):
            base = first + t * STEP
            here, there = flat.at[t % 2], turned.at[t % 2]
            for f in every:
                here[f * STEP:(f + 1) * STEP, :] = groups[t][f]
            ready = []
            if t + 1 < per:
                ready = [[spread(groups[t + 1][f], base + q) for f in every] for q in range(STEP)]
            inside = jnp.logical_and(lane_step >= base, lane_step < base + STEP)
            unit = jnp.where(lane_step == row_step + base, 1.0, 0.0)
            before.append([jnp.where(inside, unit, groups[t][f]) for f in every])
            if t + 1 == per and last < TILE:
                lefts = []
                for f in every:
                    part = split_three(jnp.concatenate([rows[f] for rows in before], 0))
                    lefts.append(jnp.transpose(jnp.concatenate([part[i] for i in (0, 0, 0, 1, 1, 2)], 0))[last:, :])
            rows = [here[pl.ds(i, fits, stride=STEP), :] for i in range(STEP)]
            cells = [[spread(rows[i], base + j) for j in range(i + 1)] for i in range(STEP)]
            within = jnp.logical_and(lane >= base, lane < base + STEP)
            for i in range(STEP):
                rows[i] = jnp.where(within, jnp.where(lane == base + i, 1.0, 0.0), rows[i])
            gains, inverses = {}, []
            for j in range(STEP):
                inverses.append(1.0 / cells[j][j])
                for i in range(j + 1, STEP):
                    gains[i, j] = cells[i][j] * inverses[j]
                for i in range(j + 1, STEP):
                    for m in range(j + 1, i + 1):
                        cells[i][m] = cells[i][m] - gains[i, j] * cells[m][j]
                for i in range(j + 1, STEP):
                    rows[i] = rows[i] - gains[i, j] * rows[j]
            rows = [value * inverse for value, inverse in zip(rows, inverses)]
            for j in reversed(range(1, STEP)):
                for i in range(j):
                    rows[i] = rows[i] - gains[j, i] * rows[j]
            for i in range(STEP):
                there[pl.ds(i, fits, stride=STEP), :] = rows[i]
            groups[t] = [there[f * STEP:(f + 1) * STEP, :] for f in every]
            if t + 1 == per:
                continue
            wide = [
                [
                    jnp.broadcast_to(there[f * STEP + q:f * STEP + q + 1, :], shape)
                    for f in every
                ]
                for q in range(STEP)
            ]
            for g in range(t + 1, per):
                if g > t + 1:
                    ready = [[spread(groups[g][f], base + q) for f in every] for q in range(STEP)]
                totals = [jnp.where(inside, 0.0, groups[g][f]) for f in every]
                for q in range(STEP):
                    totals = [totals[f] - ready[q][f] * wide[q][f] for f in every]
                groups[g] = totals
        for f in every:
            own(work, f, first, last)[...] = jnp.concatenate([rows[f] for rows in groups], 0)
            own(old, f, first, last)[...] = jnp.concatenate([rows[f] for rows in before], 0)
        if last < TILE:
            line, column = iota((SUB, TILE), 0) + first, iota((SUB, TILE), 1)
            keep = jnp.logical_or(column >= last, column // STEP <= line // STEP)
            column = iota((TILE - last, TILE), 1)
            done = jnp.logical_and(column >= first, column < last)
            rights = []
            for f in every:
                part = jnp.where(keep, jnp.concatenate([rows[f] for rows in groups], 0), 0.0)
                part = split_three(part)
                rights.append(jnp.concatenate([part[i] for i in (0, 1, 2, 0, 1, 0)], 0))
            terms = [dot_bf16(a, b) for a, b in zip(lefts, rights)]
            for f in every:
                rest = own(work, f, last)
                rest[...] = jnp.where(done, 0.0, rest[...]) - terms[f]


class Half:
    def __init__(self, ref, first, samples, markers):
        row, col = iota((TILE, TILE), 0), iota((TILE, TILE), 1)
        self.eye, self.ref, self.share = row == col, ref, 1.0 / samples
        self.totals, self.squares, self.valid = [], [], []
        for tile in range(2):
            start = half_rows("side") + SIDE * tile + 16
            total, diagonal = ref[start:start + 1, :], ref[start + 1:start + 2, :]
            middle = total * self.share
            self.totals.append(total)
            self.squares.append(diagonal * self.share - middle * middle + 1e-05)
            self.valid.append(iota((1, TILE), 1) + (first + tile) * TILE < markers)
        self.columns = [jnp.transpose(jnp.broadcast_to(t, (TILE, TILE))) for t in self.totals]

    def block(self, part, index=0):
        row = half_rows(part) + index * TILE
        return self.ref[row:row + TILE, :]

    def centred(self):
        square = self.block("square")
        turned = jnp.transpose(square)
        upper = iota((TILE, TILE), 0) <= iota((TILE, TILE), 1)
        start = half_rows("side") + SIDE + 16
        second = jnp.where(upper, turned, square)
        second = jnp.where(self.eye, self.ref[start + 1:start + 2, :], second)
        blocks = [jnp.where(upper, square, turned), self.block("between"), second]
        pairs = [(0, 0), (0, 1), (1, 1)]
        return [
            block - self.columns[i] * self.totals[j] * self.share
            for block, (i, j) in zip(blocks, pairs)
        ]

    def ridge(self, tile, penalty):
        value = jnp.where(self.valid[tile], penalty * self.squares[tile], 1.0)
        return jnp.where(self.eye, value, 0.0)

    def side(self, tile, which):
        start = half_rows("side") + SIDE * tile + 8 * which
        return self.ref[start:start + 8, :]


def lower_part(value):
    keep = iota((TILE, TILE), 1) // STEP <= iota((TILE, TILE), 0) // STEP
    return jnp.where(keep, value, 0.0)


def first_kernel(samples, markers, penalty, place, mine, lefts, rights, above, weights, work, old,
                 flat, turned):
    fits = lefts.shape[0]
    every = range(fits)
    half = Half(mine, 2 * place[2], samples, markers)
    first, between, second = half.centred()
    for f in every:
        own(work, f)[...] = first + half.ridge(0, penalty[f])
    eliminate(work, old, flat, turned, fits)
    for f in every:
        lefts[f, 0], rights[f, 0] = lower_part(own(old, f)[...]), lower_part(own(work, f)[...])
    parts = right_parts(between)
    both = products(
        [left_parts(jnp.concatenate([lefts[f, 0], rights[f, 0]], 0)) for f in every],
        [parts for f in every],
    )
    after = products(
        [left_parts(jnp.transpose(both[f][:TILE])) for f in every],
        [right_parts(both[f][TILE:]) for f in every],
    )
    for f in every:
        above[f], weights[f] = both[f][:TILE], both[f][TILE:]
        own(work, f)[...] = second - after[f] + half.ridge(1, penalty[f])
    eliminate(work, old, flat, turned, fits)
    for f in every:
        lefts[f, 1], rights[f, 1] = lower_part(own(old, f)[...]), lower_part(own(work, f)[...])


def second_kernel(
    samples, markers, penalty, place, mine, theirs, lefts, rights, above, weights,
    out, stats, centre, wide, work, old, flat, turned, rhs, scratch,
):
    fits = out.shape[0]
    every = range(fits)
    late = place[2] == 1
    halves = [Half(mine, 2 * place[2], samples, markers)]
    halves.append(Half(theirs, 2 - 2 * place[2], samples, markers))
    sums = jnp.where(late, halves[0].side(1, 0), halves[1].side(1, 0))
    counts, first, second = (sums[:, TILE - 1 - n:TILE - n] for n in range(3))
    mean = first / counts
    spread = jnp.sqrt(second / counts - mean * mean + 1e-05)
    lane = iota((TRAITS, TILE), 1)
    stats[...] = jnp.where(lane == 0, mean, jnp.where(lane == 1, spread, 0.0))
    share = 1.0 / samples

    def place_tiles(ref, index, tiles):
        for t in range(TILES):
            value = jnp.where(late, tiles[(t + 2) % TILES], tiles[t])
            cols = slice(t * TILE, (t + 1) * TILE)
            if index is None:
                ref[:, cols] = value
            else:
                ref[index, :, cols] = value

    tiles = [(halves[t // 2], t % 2) for t in range(TILES)]
    totals = [half.totals[t] for half, t in tiles]
    place_tiles(centre, None, [jnp.broadcast_to(t * share, (8, TILE)) for t in totals])
    for t, (half, tile) in enumerate(tiles):
        value = (half.side(tile, 0) - half.side(tile, 1) * mean) / spread
        value = jnp.where(half.valid[tile], value, 0.0)
        for f in every:
            rhs[f, :, t * TILE:(t + 1) * TILE] = value
    a, b = (halves[0].block("cross", n) for n in range(2))
    c, d = (halves[1].block("cross", n) for n in range(2))
    crosses = [
        [jnp.where(late, c.T, a), jnp.where(late, a.T, b)],
        [jnp.where(late, d.T, c), jnp.where(late, b.T, d)],
    ]
    rows = []
    for i in range(2):
        column = halves[0].columns[i]
        rows.append(
            jnp.concatenate(
                [crosses[i][j] - column * totals[2 + j] * share for j in range(2)], 1
            )
        )
    blocks = halves[1].centred()
    corner = [jnp.concatenate(blocks[:2], 1), blocks[2]]
    ridge = [[halves[1].ridge(t, penalty[f]) for t in range(2)] for f in every]

    def stacked(k):
        return [left_parts(jnp.concatenate([lefts[f, k], rights[f, k]], 0)) for f in every]

    def side_step(k, left, right, later):
        lo, hi = k * TILE, (k + 1) * TILE
        turned = products(
            [left_parts(rhs[f, :, lo:hi]) for f in every],
            [right_parts(jnp.transpose(left[f])) for f in every],
        )
        value = [right[f] if later is None else jnp.concatenate([right[f], later[f]], 1) for f in every]
        value = products([left_parts(turned[f]) for f in every], [right_parts(v) for v in value])
        for f in every:
            rhs[f, :, lo:hi] = value[f][:, :TILE]
            if later is not None:
                rhs[f, :, hi:] = rhs[f, :, hi:] - value[f][:, TILE:]

    parts = right_parts(rows[0])
    both = products(stacked(0), [parts for f in every])
    after = products(
        [left_parts(jnp.transpose(above[f])) for f in every],
        [right_parts(both[f][TILE:]) for f in every],
    )
    parts = [right_parts(rows[1] - after[f]) for f in every]
    more = products(stacked(1), parts)
    upper = [jnp.concatenate([both[f][:TILE], more[f][:TILE]], 0) for f in every]
    lower = [jnp.concatenate([both[f][TILE:], more[f][TILE:]], 0) for f in every]
    factors = [left_parts(jnp.transpose(upper[f])) for f in every]
    parts = [right_parts(lower[f]) for f in every]
    for i in range(2):
        cut = i * TILE
        after = products(
            [[p[cut:cut + TILE] for p in factors[f]] for f in every],
            [[p[:, cut:] for p in parts[f]] for f in every],
        )
        for f in every:
            value = corner[i] - after[f]
            block = value[:, :TILE] + ridge[f][i]
            if i == 0:
                own(work, f)[...] = block
                scratch[f, 0] = value[:, TILE:]
            else:
                scratch[f, 1] = block
    later = [jnp.concatenate([weights[f], both[f][TILE:]], 1) for f in every]
    side_step(0, [lefts[f, 0] for f in every], [rights[f, 0] for f in every], later)
    final = products(
        [left_parts(jnp.transpose(lefts[f, 0])) for f in every], [right_parts(v) for v in later]
    )
    for f in every:
        wide[f, 0, :, TILE:] = final[f]
    later = [more[f][TILE:] for f in every]
    side_step(1, [lefts[f, 1] for f in every], [rights[f, 1] for f in every], later)
    final = products(
        [left_parts(jnp.transpose(lefts[f, 1])) for f in every], [right_parts(v) for v in later]
    )
    for f in every:
        wide[f, 1, :, 2 * TILE:] = final[f]

    eliminate(work, old, flat, turned, fits)
    left = [lower_part(own(old, f)[...]) for f in every]
    right = [lower_part(own(work, f)[...]) for f in every]
    both = products(
        [left_parts(jnp.concatenate([left[f], right[f]], 0)) for f in every],
        [right_parts(scratch[f, 0]) for f in every],
    )
    later = [both[f][TILE:] for f in every]
    parts = [right_parts(v) for v in later]
    after = products([left_parts(jnp.transpose(both[f][:TILE])) for f in every], parts)
    for f in every:
        own(work, f)[...] = scratch[f, 1] - after[f]
    side_step(2, left, right, later)
    final = products([left_parts(jnp.transpose(left[f])) for f in every], parts)
    for f in every:
        wide[f, 2, :, 3 * TILE:] = final[f]
    eliminate(work, old, flat, turned, fits)
    left = [lower_part(own(old, f)[...]) for f in every]
    right = [lower_part(own(work, f)[...]) for f in every]
    side_step(3, left, right, None)
    for k in reversed(range(TILES - 1)):
        lo, hi = k * TILE, (k + 1) * TILE
        known = [dot(rhs[f, :, hi:], wide[f, k, :, hi:], NT) for f in every]
        for f in every:
            rhs[f, :, lo:hi] = rhs[f, :, lo:hi] - known[f]
    for f in every:
        place_tiles(out, f, [rhs[f, :, t * TILE:(t + 1) * TILE] for t in range(TILES)])


def predict_kernel(pairs, place, mine, other, centre, padded, out):
    odd = place[0] == 1
    rows = []
    for f in range(HALF):
        rows.append(jnp.where(odd, other[f], mine[f]))
    for f in range(HALF):
        rows.append(jnp.where(odd, mine[f], other[f]))
    if pairs:
        upper = iota(rows[0].shape, 0) < TRAITS // 2
        second = place[1] == 1
        halves = [[], []]
        for s in range(0, SLOTS, 2):
            a, b = rows[s], rows[s + 1]
            turned_a, turned_b = (pltpu.roll(v, TRAITS // 2, 0) for v in (a, b))
            low, high = jnp.where(upper, a, turned_b), jnp.where(upper, turned_a, b)
            halves[0].append(jnp.where(second, high, low))
            halves[1].append(jnp.where(second, low, high))
        rows = halves[0] + halves[1]
    weights = jnp.concatenate(rows, 0)
    count = weights.shape[0]
    shift = jnp.sum(weights * centre[0:1, :], axis=1, keepdims=True)
    parts = [part.astype(jnp.float32) for part in split_three(weights)]
    product = dot_bf16(jnp.concatenate(parts, 0).astype(jnp.bfloat16), padded[...])
    total = product[0:count] + product[count:2 * count] + product[2 * count:3 * count] - shift
    if pairs:
        out[0] = total[:count // 2]
        out[1] = total[count // 2:]
    else:
        out[...] = total


def stack_kernel(pairs, per_share, place, mine, other, stats, masked, present, folds, out):
    first = place[1] * per_share
    if pairs:
        second = place[1] == 1
        levels = jnp.concatenate(
            [jnp.where(second, other[...], mine[...]), jnp.where(second, mine[...], other[...])], 0
        )
    else:
        levels = mine[...]
    count, samples = levels.shape
    height, width = out.shape
    present = present[...]
    scaled = (masked[...] - present * stats[:, 0:1]) / stats[:, 1:2]
    pick = iota((count, TRAITS), 1) == first + iota((count, TRAITS), 0) % per_share
    spread = dot_bf16(
        jnp.where(pick, 1.0, 0.0).astype(jnp.bfloat16), present.astype(jnp.bfloat16)
    )
    masks = [
        (spread * jnp.where(folds[...] == k, 1.0, 0.0)).astype(jnp.bfloat16) for k in range(FOLDS)
    ]
    right = split_three(jnp.concatenate([levels, scaled], 0))[:2]
    none = jnp.zeros((width - FOLDS * count, samples), jnp.bfloat16)
    left = [
        jnp.concatenate([part * mask for mask in masks] + [none], 0)
        for part in split_three(levels)[:2]
    ]
    full = dot_bf16(right[1], left[0], NT) + dot_bf16(
        jnp.concatenate([right[0], right[0]], 1), jnp.concatenate([left[1], left[0]], 1), NT
    )
    row, col = iota(full.shape, 0), iota(full.shape, 1)
    trait = jnp.where(row < count, row % per_share, row - count - first)
    full = jnp.where(trait == col % per_share, full, 0.0)
    shape = (height, full.shape[0])
    level, source = iota(shape, 0), iota(shape, 1)
    slot = source // per_share
    group = jnp.where(slot % SLOTS < FITS, slot // SLOTS * FITS + slot % SLOTS, height)
    group = jnp.where(source < count, group, count // per_share // SLOTS * FITS)
    out[...] = dot(jnp.where(level == group, 1.0, 0.0), full)
    ones = jnp.ones((16, samples), jnp.bfloat16)
    squares = split_three(levels * levels)
    energy = dot_bf16(ones, squares[1], NT) + dot_bf16(ones, squares[0], NT)
    last = count // per_share // SLOTS * FITS + 1
    out[last:last + 1, 0:count] = energy[0:1, :]


def scale_kernel(per_share, blocks, samples, total, gram, cross):
    height, width = total.shape
    count = blocks * SLOTS * per_share
    levels = blocks * FITS
    value = total[...]
    energy = jnp.broadcast_to(value[levels + 1:levels + 2, 0:count], (height, count))
    level, column = iota((height, count), 0), iota((height, count), 1) // per_share
    group = jnp.where(column % SLOTS < FITS, column // SLOTS * FITS + column % SLOTS, height)
    shape = (count, width)
    source, target = iota(shape, 0), iota(shape, 1)
    by_row = dot(
        jnp.where(level == group, energy, 0.0),
        jnp.where(source % per_share == target % per_share, 1.0, 0.0),
    )
    by_column = dot(energy, jnp.where(source == target % count, 1.0, 0.0))
    root_row = jnp.where(
        iota((height, width), 0) < levels, jnp.sqrt(by_row / samples + 1e-06), 1.0
    )
    root_column = jnp.sqrt(by_column / samples + 1e-06)
    value = value / root_row / root_column * (FOLDS / samples)
    turned = jnp.transpose(value)
    shape = (FOLDS * 8, width)
    line, column = iota(shape, 0), iota(shape, 1)
    chosen = jnp.logical_and(line // 8 == column // count, line % 8 == column % per_share)
    products = jnp.where(chosen, jnp.broadcast_to(value[levels:levels + 1, :], shape), 0.0)
    shape = (width, TILE)
    slot, target = iota(shape, 0) % count // per_share, iota(shape, 1)
    group = jnp.where(slot % SLOTS < FITS, slot // SLOTS * FITS + slot % SLOTS, -1)
    products = dot(products, jnp.where(group == target, 1.0, 0.0))
    for k in range(FOLDS):
        cross[k] = products[8 * k:8 * k + per_share, 0:levels]
        for l in range(levels):
            row = k * count + (l // FITS * SLOTS + l % FITS) * per_share
            gram[k, l] = turned[row:row + per_share, 0:levels]


def swap(value, axis, mask):
    size = lax.axis_size(axis)
    return lax.ppermute(value, axis, [(i, i ^ mask) for i in range(size)])


def masks_of(axis):
    size, mask, found = lax.axis_size(axis), 1, []
    while mask < size:
        found.append(mask)
        mask *= 2
    return found


def sum_over(value, axis):
    for mask in masks_of(axis):
        value = value + swap(value, axis, mask)
    return value


def body(genotypes, traits, observed, fold_index):
    local_rows, markers = genotypes.shape
    sample_devices = lax.axis_size("samp")
    block_devices = lax.axis_size("blk")
    samples = local_rows * sample_devices
    all_markers = markers * block_devices
    width = -(-markers // TILE) * TILE
    assert width == TILES * TILE and markers + 3 <= width
    per_share = TRAITS // block_devices
    pairs = block_devices == 2
    f32 = functools.partial(jax.ShapeDtypeStruct, dtype=jnp.float32)
    position, block = lax.axis_index("samp"), lax.axis_index("blk")
    odd = position % 2
    late = position // 2 % 2
    place = jnp.stack([odd, block, late]).astype(jnp.int32)
    present = observed.T.astype(jnp.float32)
    masked = present * traits.T

    whole = lambda shape: pl.BlockSpec(shape, lambda _: (0, 0))
    packed, padded = pl.pallas_call(
        functools.partial(gram_kernel, markers),
        grid=(1,),
        out_shape=[
            f32((2 * HALF_ROWS, TILE)),
            jax.ShapeDtypeStruct((width, local_rows), jnp.bfloat16),
        ],
        in_specs=[whole((width, local_rows)), whole(masked.shape), whole(present.shape)],
        out_specs=[whole((2 * HALF_ROWS, TILE)), whole((width, local_rows))],
        compiler_params=pltpu.CompilerParams(vmem_limit_bytes=VMEM_BYTES),
        name="local_gram",
    )(genotypes.T, masked, present)
    quarters = packed.reshape(2, 2, HALF_ROWS // 2, TILE)
    up = odd == 1
    keep = jnp.where(up, quarters[:, 1], quarters[:, 0])
    value = keep + swap(jnp.where(up, quarters[:, 0], quarters[:, 1]), "samp", 1)
    keep = jnp.where(late == 1, value[1], value[0])
    value = keep + swap(jnp.where(late == 1, value[0], value[1]), "samp", 2)
    for mask in masks_of("samp")[2:]:
        value = value + swap(value, "samp", mask)
    other = swap(value, "samp", 1)
    half = jnp.concatenate([jnp.where(up, other, value), jnp.where(up, value, other)], 0)
    theirs = swap(half, "samp", 2)

    penalties = [all_markers * (1.0 - h) / h for h in HERITABILITY]
    penalties = penalties + [penalties[-1]] * (SLOTS - len(penalties))
    penalty = jnp.where(
        odd == 1,
        jnp.array(penalties[HALF:], jnp.float32),
        jnp.array(penalties[:HALF], jnp.float32),
    )
    square = (HALF, TILE, TILE)
    blocks = [pltpu.VMEM((HALF * TILE, TILE), jnp.float32)] * 2
    turns = [pltpu.VMEM((2, HALF * STEP, TILE), jnp.float32)] * 2
    started = call(
        functools.partial(first_kernel, samples, markers),
        [f32((HALF, 2, TILE, TILE)), f32((HALF, 2, TILE, TILE)), f32(square), f32(square)],
        ["smem", "smem", "vmem"],
        blocks + turns,
        "first_fits",
        cost=pl.CostEstimate(flops=4 * 10**9, bytes_accessed=2**21, transcendentals=0),
    )(penalty, place, half)
    weights, stats, centre = call(
        functools.partial(second_kernel, samples, markers),
        [f32((HALF, TRAITS, width)), f32((TRAITS, TILE)), f32((8, width))],
        ["smem", "smem"] + ["vmem"] * 6,
        [
            pltpu.VMEM((HALF, TILES, TILE, width), jnp.float32),
            *blocks,
            *turns,
            pltpu.VMEM((HALF, TRAITS, width), jnp.float32),
            pltpu.VMEM((HALF, 2, TILE, TILE), jnp.float32),
        ],
        "second_fits",
    )(penalty, place, half, theirs, *started)
    other = swap(weights, "samp", 1)

    count = SLOTS * TRAITS
    shape = (2, count // 2, local_rows) if pairs else (count, local_rows)
    predicted = call(
        functools.partial(predict_kernel, pairs),
        f32(shape),
        ["smem", "vmem", "vmem", "vmem", "vmem"],
        [],
        "predictions",
    )(place, weights, other, centre, padded)
    if pairs:
        mine, theirs = predicted[0], swap(predicted[1], "blk", 1)
    else:
        shares = predicted.reshape(SLOTS, block_devices, per_share, local_rows)
        shares = lax.all_to_all(shares, "blk", split_axis=1, concat_axis=0, tiled=True)
        mine = theirs = shares.reshape(count, local_rows)

    levels = block_devices * FITS
    height = -(-(levels + 2) // 8) * 8
    lanes = -(-FOLDS * count // TILE) * TILE
    products = call(
        functools.partial(stack_kernel, pairs, per_share),
        f32((height, lanes)),
        ["smem"] + ["vmem"] * 6,
        [],
        "stacking",
    )(place, mine, theirs, stats, masked, present, fold_index[None, :])
    products = sum_over(products, "samp")
    gram, cross = call(
        functools.partial(scale_kernel, per_share, block_devices, samples),
        [f32((FOLDS, levels, per_share, levels)), f32((FOLDS, per_share, levels))],
        ["vmem"],
        [],
        "standardize",
    )(products)
    return gram.transpose(2, 0, 1, 3), cross.transpose(1, 0, 2)


def solution(mesh):
    in_specs = (P("samp", "blk"), P("samp", None), P("samp", None), P("samp"))
    out_specs = (P("blk", None, None, None), P("blk", None, None))
    return jax.shard_map(body, mesh=mesh, in_specs=in_specs, out_specs=out_specs, check_vma=False)
```

```python
import functools
import jax
import jax.numpy as jnp
from jax import lax
from jax.experimental import pallas as pl
from jax.experimental.pallas import tpu as pltpu
from jax.sharding import PartitionSpec as P

TRAITS = 8
FOLDS = 5
HERITABILITY = (0.01, 0.25, 0.5, 0.75, 0.99)
TILE = 128
STEP = 8
SIDE = 24
SUB = 32
TILES = 4
HALF_ROWS = 4 * TILE + 2 * SIDE
FITS = len(HERITABILITY)
SLOTS = 6
HALF = SLOTS // 2
VMEM_BYTES = 32 * 1024 * 1024

NN = (((1,), (0,)), ((), ()))
NT = (((1,), (1,)), ((), ()))
TN = (((0,), (0,)), ((), ()))


def dot(a, b, dims=NN):
    return lax.dot_general(
        a, b, dims, precision=lax.Precision.HIGHEST, preferred_element_type=jnp.float32
    )


def dot_bf16(a, b, dims=NN):
    return lax.dot_general(a, b, dims, preferred_element_type=jnp.float32)


def split_three(value):
    high = value.astype(jnp.bfloat16)
    left = value - high.astype(jnp.float32)
    middle = left.astype(jnp.bfloat16)
    low = (left - middle.astype(jnp.float32)).astype(jnp.bfloat16)
    return high, middle, low


def iota(shape, dim):
    return lax.broadcasted_iota(jnp.int32, shape, dim)


def left_parts(value):
    high, middle, low = split_three(value)
    return [jnp.concatenate(pair, 1) for pair in ((low, middle), (middle, high), (high, high))]


def right_parts(value):
    high, middle, low = split_three(value)
    first = jnp.concatenate([high, middle], 0)
    return [first, first, jnp.concatenate([low, high], 0)]


def products(lefts, rights):
    totals = [dot_bf16(a[0], b[0]) for a, b in zip(lefts, rights)]
    for part in (1, 2):
        terms = [dot_bf16(a[part], b[part]) for a, b in zip(lefts, rights)]
        totals = [total + term for total, term in zip(totals, terms)]
    return totals


def half_rows(part):
    return {"square": 0, "between": TILE, "cross": 2 * TILE, "side": 4 * TILE}[part]


def call(kernel, out_shape, in_specs, scratch, name, cost=None):
    vmem = pl.BlockSpec(memory_space=pltpu.VMEM)
    smem = pl.BlockSpec(memory_space=pltpu.SMEM)
    return pl.pallas_call(
        kernel,
        out_shape=out_shape,
        in_specs=[smem if spec == "smem" else vmem for spec in in_specs],
        out_specs=jax.tree.map(lambda _: vmem, out_shape),
        scratch_shapes=scratch,
        compiler_params=pltpu.CompilerParams(vmem_limit_bytes=VMEM_BYTES),
        cost_estimate=cost,
        name=name,
    )


def gram_kernel(markers, dosage, masked, present, packed, padded):
    width, rows = padded.shape
    tiles = width // TILE
    edge = markers // 16 * 16
    padded[0:edge, :] = dosage[0:edge, :]
    tail = dosage[edge:edge + 16, :].astype(jnp.float32)
    tail = jnp.where(iota(tail.shape, 0) + edge < markers, tail, 0.0)
    padded[edge:edge + 16, :] = tail.astype(jnp.bfloat16)
    if edge + 16 < width:
        padded[edge + 16:, :] = jnp.zeros((width - edge - 16, rows), jnp.bfloat16)
    lane, line = iota((TRAITS, TILE), 1), iota((TRAITS, TILE), 0)
    upper = iota((TILE, TILE), 0) <= iota((TILE, TILE), 1)
    eye = iota((TILE, TILE), 0) == iota((TILE, TILE), 1)
    even, diagonals = None, []
    for i in range(tiles):
        here = dot_bf16(padded[i * TILE:(i + 1) * TILE, :], padded[i * TILE:, :], NT)
        top = i // 2 * HALF_ROWS
        for j in range(i + 1, tiles):
            if j // 2 == i // 2:
                row = top + half_rows("between")
            else:
                row = i * HALF_ROWS + half_rows("cross") + j % 2 * TILE
            packed[row:row + TILE, :] = here[:, (j - i) * TILE:(j - i + 1) * TILE]
        block = here[:, :TILE]
        if i % 2:
            row = top + half_rows("square")
            packed[row:row + TILE, :] = jnp.where(upper, even, block)
        even = block
        diagonals.append(jnp.sum(jnp.where(eye, block, 0.0), axis=0, keepdims=True))
    masked, present = masked[...], present[...]
    high, middle, low = (part.astype(jnp.float32) for part in split_three(masked))
    ones = jnp.ones(present.shape, jnp.float32)
    extra = jnp.concatenate([high, middle, low, present, ones, ones], 0).astype(jnp.bfloat16)
    products = dot_bf16(extra, padded[...], NT)
    sums = [jnp.sum(v, axis=1, keepdims=True) for v in (present, masked, masked * masked)]
    for i in range(tiles):
        cols = slice(i * TILE, (i + 1) * TILE)
        row = i // 2 * HALF_ROWS + half_rows("side") + i % 2 * SIDE
        total = products[0:8, cols] + products[8:16, cols] + products[16:24, cols]
        if i == tiles - 1:
            for n, value in enumerate(sums):
                total = jnp.where(lane == TILE - 1 - n, value, total)
        packed[row:row + 8, :] = total
        packed[row + 8:row + 16, :] = products[24:32, cols]
        packed[row + 16:row + 24, :] = jnp.where(line == 0, products[32:40, cols], diagonals[i])


def own(ref, fit, first=0, last=TILE):
    return ref.at[fit * TILE + first:fit * TILE + last, :]


def eliminate(work, old, flat, turned, fits):
    per, every = SUB // STEP, range(fits)
    lane, lane_step, row_step = iota((fits, TILE), 1), iota((STEP, TILE), 1), iota((STEP, TILE), 0)
    shape = (STEP, TILE)

    def spread(value, column):
        return jnp.broadcast_to(value[:, column:column + 1], value.shape)

    for first in range(0, TILE, SUB):
        last = first + SUB
        groups = [
            [own(work, f, first + g * STEP, first + (g + 1) * STEP)[...] for f in every]
            for g in range(per)
        ]
        before = []
        for t in range(per):
            base = first + t * STEP
            here, there = flat.at[t % 2], turned.at[t % 2]
            for f in every:
                here[f * STEP:(f + 1) * STEP, :] = groups[t][f]
            ready = []
            if t + 1 < per:
                ready = [[spread(groups[t + 1][f], base + q) for f in every] for q in range(STEP)]
            inside = jnp.logical_and(lane_step >= base, lane_step < base + STEP)
            unit = jnp.where(lane_step == row_step + base, 1.0, 0.0)
            before.append([jnp.where(inside, unit, groups[t][f]) for f in every])
            if t + 1 == per and last < TILE:
                lefts = []
                for f in every:
                    part = split_three(jnp.concatenate([rows[f] for rows in before], 0))
                    lefts.append(jnp.transpose(jnp.concatenate([part[i] for i in (0, 0, 0, 1, 1, 2)], 0))[last:, :])
            rows = [here[pl.ds(i, fits, stride=STEP), :] for i in range(STEP)]
            cells = [[spread(rows[i], base + j) for j in range(i + 1)] for i in range(STEP)]
            within = jnp.logical_and(lane >= base, lane < base + STEP)
            for i in range(STEP):
                rows[i] = jnp.where(within, jnp.where(lane == base + i, 1.0, 0.0), rows[i])
            gains, inverses = {}, []
            for j in range(STEP):
                inverses.append(1.0 / cells[j][j])
                for i in range(j + 1, STEP):
                    gains[i, j] = cells[i][j] * inverses[j]
                for i in range(j + 1, STEP):
                    for m in range(j + 1, i + 1):
                        cells[i][m] = cells[i][m] - gains[i, j] * cells[m][j]
                for i in range(j + 1, STEP):
                    rows[i] = rows[i] - gains[i, j] * rows[j]
            rows = [value * inverse for value, inverse in zip(rows, inverses)]
            for j in reversed(range(1, STEP)):
                for i in range(j):
                    rows[i] = rows[i] - gains[j, i] * rows[j]
            for i in range(STEP):
                there[pl.ds(i, fits, stride=STEP), :] = rows[i]
            groups[t] = [there[f * STEP:(f + 1) * STEP, :] for f in every]
            if t + 1 == per:
                continue
            wide = [
                [
                    jnp.broadcast_to(there[f * STEP + q:f * STEP + q + 1, :], shape)
                    for f in every
                ]
                for q in range(STEP)
            ]
            for g in range(t + 1, per):
                if g > t + 1:
                    ready = [[spread(groups[g][f], base + q) for f in every] for q in range(STEP)]
                totals = [jnp.where(inside, 0.0, groups[g][f]) for f in every]
                for q in range(STEP):
                    totals = [totals[f] - ready[q][f] * wide[q][f] for f in every]
                groups[g] = totals
        for f in every:
            own(work, f, first, last)[...] = jnp.concatenate([rows[f] for rows in groups], 0)
            own(old, f, first, last)[...] = jnp.concatenate([rows[f] for rows in before], 0)
        if last < TILE:
            line, column = iota((SUB, TILE), 0) + first, iota((SUB, TILE), 1)
            keep = jnp.logical_or(column >= last, column // STEP <= line // STEP)
            column = iota((TILE - last, TILE), 1)
            done = jnp.logical_and(column >= first, column < last)
            rights = []
            for f in every:
                part = jnp.where(keep, jnp.concatenate([rows[f] for rows in groups], 0), 0.0)
                part = split_three(part)
                rights.append(jnp.concatenate([part[i] for i in (0, 1, 2, 0, 1, 0)], 0))
            terms = [dot_bf16(a, b) for a, b in zip(lefts, rights)]
            for f in every:
                rest = own(work, f, last)
                rest[...] = jnp.where(done, 0.0, rest[...]) - terms[f]


class Half:
    def __init__(self, ref, first, samples, markers):
        row, col = iota((TILE, TILE), 0), iota((TILE, TILE), 1)
        self.eye, self.ref, self.share = row == col, ref, 1.0 / samples
        self.totals, self.squares, self.valid = [], [], []
        for tile in range(2):
            start = half_rows("side") + SIDE * tile + 16
            total, diagonal = ref[start:start + 1, :], ref[start + 1:start + 2, :]
            middle = total * self.share
            self.totals.append(total)
            self.squares.append(diagonal * self.share - middle * middle + 1e-05)
            self.valid.append(iota((1, TILE), 1) + (first + tile) * TILE < markers)
        self.columns = [jnp.transpose(jnp.broadcast_to(t, (TILE, TILE))) for t in self.totals]

    def block(self, part, index=0):
        row = half_rows(part) + index * TILE
        return self.ref[row:row + TILE, :]

    def centred(self):
        square = self.block("square")
        turned = jnp.transpose(square)
        upper = iota((TILE, TILE), 0) <= iota((TILE, TILE), 1)
        start = half_rows("side") + SIDE + 16
        second = jnp.where(upper, turned, square)
        second = jnp.where(self.eye, self.ref[start + 1:start + 2, :], second)
        blocks = [jnp.where(upper, square, turned), self.block("between"), second]
        pairs = [(0, 0), (0, 1), (1, 1)]
        return [
            block - self.columns[i] * self.totals[j] * self.share
            for block, (i, j) in zip(blocks, pairs)
        ]

    def ridge(self, tile, penalty):
        value = jnp.where(self.valid[tile], penalty * self.squares[tile], 1.0)
        return jnp.where(self.eye, value, 0.0)

    def side(self, tile, which):
        start = half_rows("side") + SIDE * tile + 8 * which
        return self.ref[start:start + 8, :]


def lower_part(value):
    keep = iota((TILE, TILE), 1) // STEP <= iota((TILE, TILE), 0) // STEP
    return jnp.where(keep, value, 0.0)


def first_kernel(samples, markers, penalty, place, mine, lefts, rights, above, weights, work, old,
                 flat, turned):
    fits = lefts.shape[0]
    every = range(fits)
    half = Half(mine, 2 * place[2], samples, markers)
    first, between, second = half.centred()
    for f in every:
        own(work, f)[...] = first + half.ridge(0, penalty[f])
    eliminate(work, old, flat, turned, fits)
    for f in every:
        lefts[f, 0], rights[f, 0] = lower_part(own(old, f)[...]), lower_part(own(work, f)[...])
    parts = right_parts(between)
    both = products(
        [left_parts(jnp.concatenate([lefts[f, 0], rights[f, 0]], 0)) for f in every],
        [parts for f in every],
    )
    after = products(
        [left_parts(jnp.transpose(both[f][:TILE])) for f in every],
        [right_parts(both[f][TILE:]) for f in every],
    )
    for f in every:
        above[f], weights[f] = both[f][:TILE], both[f][TILE:]
        own(work, f)[...] = second - after[f] + half.ridge(1, penalty[f])
    eliminate(work, old, flat, turned, fits)
    for f in every:
        lefts[f, 1], rights[f, 1] = lower_part(own(old, f)[...]), lower_part(own(work, f)[...])


def second_kernel(
    samples, markers, penalty, place, mine, theirs, lefts, rights, above, weights,
    out, stats, centre, wide, work, old, flat, turned, rhs, scratch,
):
    fits = out.shape[0]
    every = range(fits)
    late = place[2] == 1
    halves = [Half(mine, 2 * place[2], samples, markers)]
    halves.append(Half(theirs, 2 - 2 * place[2], samples, markers))
    sums = jnp.where(late, halves[0].side(1, 0), halves[1].side(1, 0))
    counts, first, second = (sums[:, TILE - 1 - n:TILE - n] for n in range(3))
    mean = first / counts
    spread = jnp.sqrt(second / counts - mean * mean + 1e-05)
    lane = iota((TRAITS, TILE), 1)
    stats[...] = jnp.where(lane == 0, mean, jnp.where(lane == 1, spread, 0.0))
    share = 1.0 / samples

    def place_tiles(ref, index, tiles):
        for t in range(TILES):
            value = jnp.where(late, tiles[(t + 2) % TILES], tiles[t])
            cols = slice(t * TILE, (t + 1) * TILE)
            if index is None:
                ref[:, cols] = value
            else:
                ref[index, :, cols] = value

    tiles = [(halves[t // 2], t % 2) for t in range(TILES)]
    totals = [half.totals[t] for half, t in tiles]
    place_tiles(centre, None, [jnp.broadcast_to(t * share, (8, TILE)) for t in totals])
    for t, (half, tile) in enumerate(tiles):
        value = (half.side(tile, 0) - half.side(tile, 1) * mean) / spread
        value = jnp.where(half.valid[tile], value, 0.0)
        for f in every:
            rhs[f, :, t * TILE:(t + 1) * TILE] = value
    a, b = (halves[0].block("cross", n) for n in range(2))
    c, d = (halves[1].block("cross", n) for n in range(2))
    crosses = [
        [jnp.where(late, c.T, a), jnp.where(late, a.T, b)],
        [jnp.where(late, d.T, c), jnp.where(late, b.T, d)],
    ]
    rows = []
    for i in range(2):
        column = halves[0].columns[i]
        rows.append(
            jnp.concatenate(
                [crosses[i][j] - column * totals[2 + j] * share for j in range(2)], 1
            )
        )
    blocks = halves[1].centred()
    corner = [jnp.concatenate(blocks[:2], 1), blocks[2]]
    ridge = [[halves[1].ridge(t, penalty[f]) for t in range(2)] for f in every]

    def stacked(k):
        return [left_parts(jnp.concatenate([lefts[f, k], rights[f, k]], 0)) for f in every]

    def side_step(k, left, right, later):
        lo, hi = k * TILE, (k + 1) * TILE
        turned = products(
            [left_parts(rhs[f, :, lo:hi]) for f in every],
            [right_parts(jnp.transpose(left[f])) for f in every],
        )
        value = [right[f] if later is None else jnp.concatenate([right[f], later[f]], 1) for f in every]
        value = products([left_parts(turned[f]) for f in every], [right_parts(v) for v in value])
        for f in every:
            rhs[f, :, lo:hi] = value[f][:, :TILE]
            if later is not None:
                rhs[f, :, hi:] = rhs[f, :, hi:] - value[f][:, TILE:]

    parts = right_parts(rows[0])
    both = products(stacked(0), [parts for f in every])
    after = products(
        [left_parts(jnp.transpose(above[f])) for f in every],
        [right_parts(both[f][TILE:]) for f in every],
    )
    parts = [right_parts(rows[1] - after[f]) for f in every]
    more = products(stacked(1), parts)
    upper = [jnp.concatenate([both[f][:TILE], more[f][:TILE]], 0) for f in every]
    lower = [jnp.concatenate([both[f][TILE:], more[f][TILE:]], 0) for f in every]
    factors = [left_parts(jnp.transpose(upper[f])) for f in every]
    parts = [right_parts(lower[f]) for f in every]
    for i in range(2):
        cut = i * TILE
        after = products(
            [[p[cut:cut + TILE] for p in factors[f]] for f in every],
            [[p[:, cut:] for p in parts[f]] for f in every],
        )
        for f in every:
            value = corner[i] - after[f]
            block = value[:, :TILE] + ridge[f][i]
            if i == 0:
                own(work, f)[...] = block
                scratch[f, 0] = value[:, TILE:]
            else:
                scratch[f, 1] = block
    later = [jnp.concatenate([weights[f], both[f][TILE:]], 1) for f in every]
    side_step(0, [lefts[f, 0] for f in every], [rights[f, 0] for f in every], later)
    final = products(
        [left_parts(jnp.transpose(lefts[f, 0])) for f in every], [right_parts(v) for v in later]
    )
    for f in every:
        wide[f, 0, :, TILE:] = final[f]
    later = [more[f][TILE:] for f in every]
    side_step(1, [lefts[f, 1] for f in every], [rights[f, 1] for f in every], later)
    final = products(
        [left_parts(jnp.transpose(lefts[f, 1])) for f in every], [right_parts(v) for v in later]
    )
    for f in every:
        wide[f, 1, :, 2 * TILE:] = final[f]

    eliminate(work, old, flat, turned, fits)
    left = [lower_part(own(old, f)[...]) for f in every]
    right = [lower_part(own(work, f)[...]) for f in every]
    both = products(
        [left_parts(jnp.concatenate([left[f], right[f]], 0)) for f in every],
        [right_parts(scratch[f, 0]) for f in every],
    )
    later = [both[f][TILE:] for f in every]
    parts = [right_parts(v) for v in later]
    after = products([left_parts(jnp.transpose(both[f][:TILE])) for f in every], parts)
    for f in every:
        own(work, f)[...] = scratch[f, 1] - after[f]
    side_step(2, left, right, later)
    final = products([left_parts(jnp.transpose(left[f])) for f in every], parts)
    for f in every:
        wide[f, 2, :, 3 * TILE:] = final[f]
    eliminate(work, old, flat, turned, fits)
    left = [lower_part(own(old, f)[...]) for f in every]
    right = [lower_part(own(work, f)[...]) for f in every]
    side_step(3, left, right, None)
    for k in reversed(range(TILES - 1)):
        lo, hi = k * TILE, (k + 1) * TILE
        known = [right_parts(jnp.transpose(wide[f, k, :, hi:])) for f in every]
        known = products([left_parts(rhs[f, :, hi:]) for f in every], known)
        for f in every:
            rhs[f, :, lo:hi] = rhs[f, :, lo:hi] - known[f]
    for f in every:
        place_tiles(out, f, [rhs[f, :, t * TILE:(t + 1) * TILE] for t in range(TILES)])


def predict_kernel(pairs, place, mine, other, centre, padded, out):
    odd = place[0] == 1
    rows = []
    for f in range(HALF):
        rows.append(jnp.where(odd, other[f], mine[f]))
    for f in range(HALF):
        rows.append(jnp.where(odd, mine[f], other[f]))
    if pairs:
        upper = iota(rows[0].shape, 0) < TRAITS // 2
        second = place[1] == 1
        halves = [[], []]
        for s in range(0, SLOTS, 2):
            a, b = rows[s], rows[s + 1]
            turned_a, turned_b = (pltpu.roll(v, TRAITS // 2, 0) for v in (a, b))
            low, high = jnp.where(upper, a, turned_b), jnp.where(upper, turned_a, b)
            halves[0].append(jnp.where(second, high, low))
            halves[1].append(jnp.where(second, low, high))
        rows = halves[0] + halves[1]
    weights = jnp.concatenate(rows, 0)
    count = weights.shape[0]
    shift = jnp.sum(weights * centre[0:1, :], axis=1, keepdims=True)
    parts = [part.astype(jnp.float32) for part in split_three(weights)]
    product = dot_bf16(jnp.concatenate(parts, 0).astype(jnp.bfloat16), padded[...])
    total = product[0:count] + product[count:2 * count] + product[2 * count:3 * count] - shift
    if pairs:
        out[0] = total[:count // 2]
        out[1] = total[count // 2:]
    else:
        out[...] = total


def stack_kernel(pairs, per_share, place, mine, other, stats, masked, present, folds, out):
    first = place[1] * per_share
    if pairs:
        second = place[1] == 1
        levels = jnp.concatenate(
            [jnp.where(second, other[...], mine[...]), jnp.where(second, mine[...], other[...])], 0
        )
    else:
        levels = mine[...]
    count, samples = levels.shape
    height, width = out.shape
    present = present[...]
    scaled = (masked[...] - present * stats[:, 0:1]) / stats[:, 1:2]
    pick = iota((count, TRAITS), 1) == first + iota((count, TRAITS), 0) % per_share
    spread = dot_bf16(
        jnp.where(pick, 1.0, 0.0).astype(jnp.bfloat16), present.astype(jnp.bfloat16)
    )
    masks = [
        (spread * jnp.where(folds[...] == k, 1.0, 0.0)).astype(jnp.bfloat16) for k in range(FOLDS)
    ]
    right = split_three(jnp.concatenate([levels, scaled], 0))[:2]
    none = jnp.zeros((width - FOLDS * count, samples), jnp.bfloat16)
    left = [
        jnp.concatenate([part * mask for mask in masks] + [none], 0)
        for part in split_three(levels)[:2]
    ]
    full = dot_bf16(right[1], left[0], NT) + dot_bf16(
        jnp.concatenate([right[0], right[0]], 1), jnp.concatenate([left[1], left[0]], 1), NT
    )
    row, col = iota(full.shape, 0), iota(full.shape, 1)
    trait = jnp.where(row < count, row % per_share, row - count - first)
    full = jnp.where(trait == col % per_share, full, 0.0)
    shape = (height, full.shape[0])
    level, source = iota(shape, 0), iota(shape, 1)
    slot = source // per_share
    group = jnp.where(slot % SLOTS < FITS, slot // SLOTS * FITS + slot % SLOTS, height)
    group = jnp.where(source < count, group, count // per_share // SLOTS * FITS)
    out[...] = dot(jnp.where(level == group, 1.0, 0.0), full)
    ones = jnp.ones((16, samples), jnp.bfloat16)
    squares = split_three(levels * levels)
    energy = dot_bf16(ones, squares[1], NT) + dot_bf16(ones, squares[0], NT)
    last = count // per_share // SLOTS * FITS + 1
    out[last:last + 1, 0:count] = energy[0:1, :]


def scale_kernel(per_share, blocks, samples, total, gram, cross):
    height, width = total.shape
    count = blocks * SLOTS * per_share
    levels = blocks * FITS
    value = total[...]
    energy = jnp.broadcast_to(value[levels + 1:levels + 2, 0:count], (height, count))
    level, column = iota((height, count), 0), iota((height, count), 1) // per_share
    group = jnp.where(column % SLOTS < FITS, column // SLOTS * FITS + column % SLOTS, height)
    shape = (count, width)
    source, target = iota(shape, 0), iota(shape, 1)
    by_row = dot(
        jnp.where(level == group, energy, 0.0),
        jnp.where(source % per_share == target % per_share, 1.0, 0.0),
    )
    by_column = dot(energy, jnp.where(source == target % count, 1.0, 0.0))
    root_row = jnp.where(
        iota((height, width), 0) < levels, jnp.sqrt(by_row / samples + 1e-06), 1.0
    )
    root_column = jnp.sqrt(by_column / samples + 1e-06)
    value = value / root_row / root_column * (FOLDS / samples)
    turned = jnp.transpose(value)
    shape = (FOLDS * 8, width)
    line, column = iota(shape, 0), iota(shape, 1)
    chosen = jnp.logical_and(line // 8 == column // count, line % 8 == column % per_share)
    products = jnp.where(chosen, jnp.broadcast_to(value[levels:levels + 1, :], shape), 0.0)
    shape = (width, TILE)
    slot, target = iota(shape, 0) % count // per_share, iota(shape, 1)
    group = jnp.where(slot % SLOTS < FITS, slot // SLOTS * FITS + slot % SLOTS, -1)
    products = dot(products, jnp.where(group == target, 1.0, 0.0))
    for k in range(FOLDS):
        cross[k] = products[8 * k:8 * k + per_share, 0:levels]
        for l in range(levels):
            row = k * count + (l // FITS * SLOTS + l % FITS) * per_share
            gram[k, l] = turned[row:row + per_share, 0:levels]


def swap(value, axis, mask):
    size = lax.axis_size(axis)
    return lax.ppermute(value, axis, [(i, i ^ mask) for i in range(size)])


def masks_of(axis):
    size, mask, found = lax.axis_size(axis), 1, []
    while mask < size:
        found.append(mask)
        mask *= 2
    return found


def sum_over(value, axis):
    for mask in masks_of(axis):
        value = value + swap(value, axis, mask)
    return value


def body(genotypes, traits, observed, fold_index):
    local_rows, markers = genotypes.shape
    sample_devices = lax.axis_size("samp")
    block_devices = lax.axis_size("blk")
    samples = local_rows * sample_devices
    all_markers = markers * block_devices
    width = -(-markers // TILE) * TILE
    assert width == TILES * TILE and markers + 3 <= width
    per_share = TRAITS // block_devices
    pairs = block_devices == 2
    f32 = functools.partial(jax.ShapeDtypeStruct, dtype=jnp.float32)
    position, block = lax.axis_index("samp"), lax.axis_index("blk")
    odd = position % 2
    late = position // 2 % 2
    place = jnp.stack([odd, block, late]).astype(jnp.int32)
    present = observed.T.astype(jnp.float32)
    masked = present * traits.T

    whole = lambda shape: pl.BlockSpec(shape, lambda _: (0, 0))
    packed, padded = pl.pallas_call(
        functools.partial(gram_kernel, markers),
        grid=(1,),
        out_shape=[
            f32((2 * HALF_ROWS, TILE)),
            jax.ShapeDtypeStruct((width, local_rows), jnp.bfloat16),
        ],
        in_specs=[whole((width, local_rows)), whole(masked.shape), whole(present.shape)],
        out_specs=[whole((2 * HALF_ROWS, TILE)), whole((width, local_rows))],
        compiler_params=pltpu.CompilerParams(vmem_limit_bytes=VMEM_BYTES),
        name="local_gram",
    )(genotypes.T, masked, present)
    quarters = packed.reshape(2, 2, HALF_ROWS // 2, TILE)
    up = odd == 1
    keep = jnp.where(up, quarters[:, 1], quarters[:, 0])
    value = keep + swap(jnp.where(up, quarters[:, 0], quarters[:, 1]), "samp", 1)
    keep = jnp.where(late == 1, value[1], value[0])
    value = keep + swap(jnp.where(late == 1, value[0], value[1]), "samp", 2)
    for mask in masks_of("samp")[2:]:
        value = value + swap(value, "samp", mask)
    other = swap(value, "samp", 1)
    half = jnp.concatenate([jnp.where(up, other, value), jnp.where(up, value, other)], 0)
    theirs = swap(half, "samp", 2)

    penalties = [all_markers * (1.0 - h) / h for h in HERITABILITY]
    penalties = penalties + [penalties[-1]] * (SLOTS - len(penalties))
    penalty = jnp.where(
        odd == 1,
        jnp.array(penalties[HALF:], jnp.float32),
        jnp.array(penalties[:HALF], jnp.float32),
    )
    square = (HALF, TILE, TILE)
    blocks = [pltpu.VMEM((HALF * TILE, TILE), jnp.float32)] * 2
    turns = [pltpu.VMEM((2, HALF * STEP, TILE), jnp.float32)] * 2
    started = call(
        functools.partial(first_kernel, samples, markers),
        [f32((HALF, 2, TILE, TILE)), f32((HALF, 2, TILE, TILE)), f32(square), f32(square)],
        ["smem", "smem", "vmem"],
        blocks + turns,
        "first_fits",
        cost=pl.CostEstimate(flops=4 * 10**9, bytes_accessed=2**21, transcendentals=0),
    )(penalty, place, half)
    weights, stats, centre = call(
        functools.partial(second_kernel, samples, markers),
        [f32((HALF, TRAITS, width)), f32((TRAITS, TILE)), f32((8, width))],
        ["smem", "smem"] + ["vmem"] * 6,
        [
            pltpu.VMEM((HALF, TILES, TILE, width), jnp.float32),
            *blocks,
            *turns,
            pltpu.VMEM((HALF, TRAITS, width), jnp.float32),
            pltpu.VMEM((HALF, 2, TILE, TILE), jnp.float32),
        ],
        "second_fits",
    )(penalty, place, half, theirs, *started)
    other = swap(weights, "samp", 1)

    count = SLOTS * TRAITS
    shape = (2, count // 2, local_rows) if pairs else (count, local_rows)
    predicted = call(
        functools.partial(predict_kernel, pairs),
        f32(shape),
        ["smem", "vmem", "vmem", "vmem", "vmem"],
        [],
        "predictions",
    )(place, weights, other, centre, padded)
    if pairs:
        mine, theirs = predicted[0], swap(predicted[1], "blk", 1)
    else:
        shares = predicted.reshape(SLOTS, block_devices, per_share, local_rows)
        shares = lax.all_to_all(shares, "blk", split_axis=1, concat_axis=0, tiled=True)
        mine = theirs = shares.reshape(count, local_rows)

    levels = block_devices * FITS
    height = -(-(levels + 2) // 8) * 8
    lanes = -(-FOLDS * count // TILE) * TILE
    products = call(
        functools.partial(stack_kernel, pairs, per_share),
        f32((height, lanes)),
        ["smem"] + ["vmem"] * 6,
        [],
        "stacking",
    )(place, mine, theirs, stats, masked, present, fold_index[None, :])
    products = sum_over(products, "samp")
    gram, cross = call(
        functools.partial(scale_kernel, per_share, block_devices, samples),
        [f32((FOLDS, levels, per_share, levels)), f32((FOLDS, per_share, levels))],
        ["vmem"],
        [],
        "standardize",
    )(products)
    return gram.transpose(2, 0, 1, 3), cross.transpose(1, 0, 2)


def solution(mesh):
    in_specs = (P("samp", "blk"), P("samp", None), P("samp", None), P("samp"))
    out_specs = (P("blk", None, None, None), P("blk", None, None))
    return jax.shard_map(body, mesh=mesh, in_specs=in_specs, out_specs=out_specs, check_vma=False)
```

```python
import functools
import jax
import jax.numpy as jnp
from jax import lax
from jax.experimental import pallas as pl
from jax.experimental.pallas import tpu as pltpu
from jax.sharding import PartitionSpec as P

TRAITS = 8
FOLDS = 5
HERITABILITY = (0.01, 0.25, 0.5, 0.75, 0.99)
TILE = 128
STEP = 8
SIDE = 24
SUB = 32
TILES = 4
HALF_ROWS = 4 * TILE + 2 * SIDE
FITS = len(HERITABILITY)
SLOTS = 6
HALF = SLOTS // 2
VMEM_BYTES = 32 * 1024 * 1024

NN = (((1,), (0,)), ((), ()))
NT = (((1,), (1,)), ((), ()))
TN = (((0,), (0,)), ((), ()))


def dot(a, b, dims=NN):
    return lax.dot_general(
        a, b, dims, precision=lax.Precision.HIGHEST, preferred_element_type=jnp.float32
    )


def dot_bf16(a, b, dims=NN):
    return lax.dot_general(a, b, dims, preferred_element_type=jnp.float32)


def split_three(value):
    high = value.astype(jnp.bfloat16)
    left = value - high.astype(jnp.float32)
    middle = left.astype(jnp.bfloat16)
    low = (left - middle.astype(jnp.float32)).astype(jnp.bfloat16)
    return high, middle, low


def iota(shape, dim):
    return lax.broadcasted_iota(jnp.int32, shape, dim)


def left_parts(value):
    high, middle, low = split_three(value)
    return [jnp.concatenate(pair, 1) for pair in ((low, middle), (middle, high), (high, high))]


def right_parts(value):
    high, middle, low = split_three(value)
    first = jnp.concatenate([high, middle], 0)
    return [first, first, jnp.concatenate([low, high], 0)]


def products(lefts, rights):
    totals = [dot_bf16(a[0], b[0]) for a, b in zip(lefts, rights)]
    for part in (1, 2):
        terms = [dot_bf16(a[part], b[part]) for a, b in zip(lefts, rights)]
        totals = [total + term for total, term in zip(totals, terms)]
    return totals


def half_rows(part):
    return {"square": 0, "between": TILE, "cross": 2 * TILE, "side": 4 * TILE}[part]


def call(kernel, out_shape, in_specs, scratch, name, cost=None):
    vmem = pl.BlockSpec(memory_space=pltpu.VMEM)
    smem = pl.BlockSpec(memory_space=pltpu.SMEM)
    return pl.pallas_call(
        kernel,
        out_shape=out_shape,
        in_specs=[smem if spec == "smem" else vmem for spec in in_specs],
        out_specs=jax.tree.map(lambda _: vmem, out_shape),
        scratch_shapes=scratch,
        compiler_params=pltpu.CompilerParams(vmem_limit_bytes=VMEM_BYTES),
        cost_estimate=cost,
        name=name,
    )


def gram_kernel(markers, dosage, masked, present, packed, padded):
    width, rows = padded.shape
    tiles = width // TILE
    edge = markers // 16 * 16
    padded[0:edge, :] = dosage[0:edge, :]
    tail = dosage[edge:edge + 16, :].astype(jnp.float32)
    tail = jnp.where(iota(tail.shape, 0) + edge < markers, tail, 0.0)
    padded[edge:edge + 16, :] = tail.astype(jnp.bfloat16)
    if edge + 16 < width:
        padded[edge + 16:, :] = jnp.zeros((width - edge - 16, rows), jnp.bfloat16)
    lane, line = iota((TRAITS, TILE), 1), iota((TRAITS, TILE), 0)
    upper = iota((TILE, TILE), 0) <= iota((TILE, TILE), 1)
    eye = iota((TILE, TILE), 0) == iota((TILE, TILE), 1)
    even, diagonals = None, []
    for i in range(tiles):
        here = dot_bf16(padded[i * TILE:(i + 1) * TILE, :], padded[i * TILE:, :], NT)
        top = i // 2 * HALF_ROWS
        for j in range(i + 1, tiles):
            if j // 2 == i // 2:
                row = top + half_rows("between")
            else:
                row = i * HALF_ROWS + half_rows("cross") + j % 2 * TILE
            packed[row:row + TILE, :] = here[:, (j - i) * TILE:(j - i + 1) * TILE]
        block = here[:, :TILE]
        if i % 2:
            row = top + half_rows("square")
            packed[row:row + TILE, :] = jnp.where(upper, even, block)
        even = block
        diagonals.append(jnp.sum(jnp.where(eye, block, 0.0), axis=0, keepdims=True))
    masked, present = masked[...], present[...]
    high, middle, low = (part.astype(jnp.float32) for part in split_three(masked))
    ones = jnp.ones(present.shape, jnp.float32)
    extra = jnp.concatenate([high, middle, low, present, ones, ones], 0).astype(jnp.bfloat16)
    products = dot_bf16(extra, padded[...], NT)
    sums = [jnp.sum(v, axis=1, keepdims=True) for v in (present, masked, masked * masked)]
    for i in range(tiles):
        cols = slice(i * TILE, (i + 1) * TILE)
        row = i // 2 * HALF_ROWS + half_rows("side") + i % 2 * SIDE
        total = products[0:8, cols] + products[8:16, cols] + products[16:24, cols]
        if i == tiles - 1:
            for n, value in enumerate(sums):
                total = jnp.where(lane == TILE - 1 - n, value, total)
        packed[row:row + 8, :] = total
        packed[row + 8:row + 16, :] = products[24:32, cols]
        packed[row + 16:row + 24, :] = jnp.where(line == 0, products[32:40, cols], diagonals[i])


def own(ref, fit, first=0, last=TILE):
    return ref.at[fit * TILE + first:fit * TILE + last, :]


def eliminate(work, old, flat, turned, fits):
    per, every = SUB // STEP, range(fits)
    lane, lane_step, row_step = iota((fits, TILE), 1), iota((STEP, TILE), 1), iota((STEP, TILE), 0)
    shape = (STEP, TILE)

    def spread(value, column):
        return jnp.broadcast_to(value[:, column:column + 1], value.shape)

    for first in range(0, TILE, SUB):
        last = first + SUB
        groups = [
            [own(work, f, first + g * STEP, first + (g + 1) * STEP)[...] for f in every]
            for g in range(per)
        ]
        before = []
        for t in range(per):
            base = first + t * STEP
            here, there = flat.at[t % 2], turned.at[t % 2]
            for f in every:
                here[f * STEP:(f + 1) * STEP, :] = groups[t][f]
            ready = []
            if t + 1 < per:
                ready = [[spread(groups[t + 1][f], base + q) for f in every] for q in range(STEP)]
            inside = jnp.logical_and(lane_step >= base, lane_step < base + STEP)
            unit = jnp.where(lane_step == row_step + base, 1.0, 0.0)
            before.append([jnp.where(inside, unit, groups[t][f]) for f in every])
            if t + 1 == per and last < TILE:
                lefts = []
                for f in every:
                    part = split_three(jnp.concatenate([rows[f] for rows in before], 0))
                    lefts.append(jnp.transpose(jnp.concatenate([part[i] for i in (0, 0, 0, 1, 1, 2)], 0))[last:, :])
            rows = [here[pl.ds(i, fits, stride=STEP), :] for i in range(STEP)]
            cells = [[spread(rows[i], base + j) for j in range(i + 1)] for i in range(STEP)]
            within = jnp.logical_and(lane >= base, lane < base + STEP)
            for i in range(STEP):
                rows[i] = jnp.where(within, jnp.where(lane == base + i, 1.0, 0.0), rows[i])
            gains, inverses = {}, []
            for j in range(STEP):
                inverses.append(1.0 / cells[j][j])
                for i in range(j + 1, STEP):
                    gains[i, j] = cells[i][j] * inverses[j]
                for i in range(j + 1, STEP):
                    for m in range(j + 1, i + 1):
                        cells[i][m] = cells[i][m] - gains[i, j] * cells[m][j]
                for i in range(j + 1, STEP):
                    rows[i] = rows[i] - gains[i, j] * rows[j]
            rows = [value * inverse for value, inverse in zip(rows, inverses)]
            for j in reversed(range(1, STEP)):
                for i in range(j):
                    rows[i] = rows[i] - gains[j, i] * rows[j]
            for i in range(STEP):
                there[pl.ds(i, fits, stride=STEP), :] = rows[i]
            groups[t] = [there[f * STEP:(f + 1) * STEP, :] for f in every]
            if t + 1 == per:
                continue
            wide = [
                [
                    jnp.broadcast_to(there[f * STEP + q:f * STEP + q + 1, :], shape)
                    for f in every
                ]
                for q in range(STEP)
            ]
            for g in range(t + 1, per):
                if g > t + 1:
                    ready = [[spread(groups[g][f], base + q) for f in every] for q in range(STEP)]
                totals = [jnp.where(inside, 0.0, groups[g][f]) for f in every]
                for q in range(STEP):
                    totals = [totals[f] - ready[q][f] * wide[q][f] for f in every]
                groups[g] = totals
        for f in every:
            own(work, f, first, last)[...] = jnp.concatenate([rows[f] for rows in groups], 0)
            own(old, f, first, last)[...] = jnp.concatenate([rows[f] for rows in before], 0)
        if last < TILE:
            line, column = iota((SUB, TILE), 0) + first, iota((SUB, TILE), 1)
            keep = jnp.logical_or(column >= last, column // STEP <= line // STEP)
            column = iota((TILE - last, TILE), 1)
            done = jnp.logical_and(column >= first, column < last)
            rights = []
            for f in every:
                part = jnp.where(keep, jnp.concatenate([rows[f] for rows in groups], 0), 0.0)
                part = split_three(part)
                rights.append(jnp.concatenate([part[i] for i in (0, 1, 2, 0, 1, 0)], 0))
            terms = [dot_bf16(a, b) for a, b in zip(lefts, rights)]
            for f in every:
                rest = own(work, f, last)
                rest[...] = jnp.where(done, 0.0, rest[...]) - terms[f]


class Half:
    def __init__(self, ref, first, samples, markers):
        row, col = iota((TILE, TILE), 0), iota((TILE, TILE), 1)
        self.eye, self.ref, self.share = row == col, ref, 1.0 / samples
        self.totals, self.squares, self.valid = [], [], []
        for tile in range(2):
            start = half_rows("side") + SIDE * tile + 16
            total, diagonal = ref[start:start + 1, :], ref[start + 1:start + 2, :]
            middle = total * self.share
            self.totals.append(total)
            self.squares.append(diagonal * self.share - middle * middle + 1e-05)
            self.valid.append(iota((1, TILE), 1) + (first + tile) * TILE < markers)
        self.columns = [jnp.transpose(jnp.broadcast_to(t, (TILE, TILE))) for t in self.totals]

    def block(self, part, index=0):
        row = half_rows(part) + index * TILE
        return self.ref[row:row + TILE, :]

    def centred(self):
        square = self.block("square")
        turned = jnp.transpose(square)
        upper = iota((TILE, TILE), 0) <= iota((TILE, TILE), 1)
        start = half_rows("side") + SIDE + 16
        second = jnp.where(upper, turned, square)
        second = jnp.where(self.eye, self.ref[start + 1:start + 2, :], second)
        blocks = [jnp.where(upper, square, turned), self.block("between"), second]
        pairs = [(0, 0), (0, 1), (1, 1)]
        return [
            block - self.columns[i] * self.totals[j] * self.share
            for block, (i, j) in zip(blocks, pairs)
        ]

    def ridge(self, tile, penalty):
        value = jnp.where(self.valid[tile], penalty * self.squares[tile], 1.0)
        return jnp.where(self.eye, value, 0.0)

    def side(self, tile, which):
        start = half_rows("side") + SIDE * tile + 8 * which
        return self.ref[start:start + 8, :]


def lower_part(value):
    keep = iota((TILE, TILE), 1) // STEP <= iota((TILE, TILE), 0) // STEP
    return jnp.where(keep, value, 0.0)


def first_kernel(samples, markers, penalty, place, mine, lefts, rights, above, weights, work, old,
                 flat, turned):
    fits = lefts.shape[0]
    every = range(fits)
    half = Half(mine, 2 * place[2], samples, markers)
    first, between, second = half.centred()
    for f in every:
        own(work, f)[...] = first + half.ridge(0, penalty[f])
    eliminate(work, old, flat, turned, fits)
    for f in every:
        lefts[f, 0], rights[f, 0] = lower_part(own(old, f)[...]), lower_part(own(work, f)[...])
    parts = right_parts(between)
    both = products(
        [left_parts(jnp.concatenate([lefts[f, 0], rights[f, 0]], 0)) for f in every],
        [parts for f in every],
    )
    after = products(
        [left_parts(jnp.transpose(both[f][:TILE])) for f in every],
        [right_parts(both[f][TILE:]) for f in every],
    )
    for f in every:
        above[f], weights[f] = both[f][:TILE], both[f][TILE:]
        own(work, f)[...] = second - after[f] + half.ridge(1, penalty[f])
    eliminate(work, old, flat, turned, fits)
    for f in every:
        lefts[f, 1], rights[f, 1] = lower_part(own(old, f)[...]), lower_part(own(work, f)[...])


def second_kernel(
    samples, markers, penalty, place, mine, theirs, lefts, rights, above, weights,
    out, stats, centre, wide, work, old, flat, turned, rhs, scratch,
):
    fits = out.shape[0]
    every = range(fits)
    late = place[2] == 1
    halves = [Half(mine, 2 * place[2], samples, markers)]
    halves.append(Half(theirs, 2 - 2 * place[2], samples, markers))
    sums = jnp.where(late, halves[0].side(1, 0), halves[1].side(1, 0))
    counts, first, second = (sums[:, TILE - 1 - n:TILE - n] for n in range(3))
    mean = first / counts
    spread = jnp.sqrt(second / counts - mean * mean + 1e-05)
    lane = iota((TRAITS, TILE), 1)
    stats[...] = jnp.where(lane == 0, mean, jnp.where(lane == 1, spread, 0.0))
    share = 1.0 / samples

    def place_tiles(ref, index, tiles):
        for t in range(TILES):
            value = jnp.where(late, tiles[(t + 2) % TILES], tiles[t])
            cols = slice(t * TILE, (t + 1) * TILE)
            if index is None:
                ref[:, cols] = value
            else:
                ref[index, :, cols] = value

    tiles = [(halves[t // 2], t % 2) for t in range(TILES)]
    totals = [half.totals[t] for half, t in tiles]
    place_tiles(centre, None, [jnp.broadcast_to(t * share, (8, TILE)) for t in totals])
    for t, (half, tile) in enumerate(tiles):
        value = (half.side(tile, 0) - half.side(tile, 1) * mean) / spread
        value = jnp.where(half.valid[tile], value, 0.0)
        for f in every:
            rhs[f, :, t * TILE:(t + 1) * TILE] = value
    a, b = (halves[0].block("cross", n) for n in range(2))
    c, d = (halves[1].block("cross", n) for n in range(2))
    crosses = [
        [jnp.where(late, c.T, a), jnp.where(late, a.T, b)],
        [jnp.where(late, d.T, c), jnp.where(late, b.T, d)],
    ]
    rows = []
    for i in range(2):
        column = halves[0].columns[i]
        rows.append(
            jnp.concatenate(
                [crosses[i][j] - column * totals[2 + j] * share for j in range(2)], 1
            )
        )
    blocks = halves[1].centred()
    corner = [jnp.concatenate(blocks[:2], 1), blocks[2]]
    ridge = [[halves[1].ridge(t, penalty[f]) for t in range(2)] for f in every]

    def stacked(k):
        return [left_parts(jnp.concatenate([lefts[f, k], rights[f, k]], 0)) for f in every]

    def side_step(k, left, right, later):
        lo, hi = k * TILE, (k + 1) * TILE
        turned = products(
            [left_parts(rhs[f, :, lo:hi]) for f in every],
            [right_parts(jnp.transpose(left[f])) for f in every],
        )
        value = [right[f] if later is None else jnp.concatenate([right[f], later[f]], 1) for f in every]
        value = products([left_parts(turned[f]) for f in every], [right_parts(v) for v in value])
        for f in every:
            rhs[f, :, lo:hi] = value[f][:, :TILE]
            if later is not None:
                rhs[f, :, hi:] = rhs[f, :, hi:] - value[f][:, TILE:]

    parts = right_parts(rows[0])
    both = products(stacked(0), [parts for f in every])
    after = products(
        [left_parts(jnp.transpose(above[f])) for f in every],
        [right_parts(both[f][TILE:]) for f in every],
    )
    parts = [right_parts(rows[1] - after[f]) for f in every]
    more = products(stacked(1), parts)
    upper = [jnp.concatenate([both[f][:TILE], more[f][:TILE]], 0) for f in every]
    lower = [jnp.concatenate([both[f][TILE:], more[f][TILE:]], 0) for f in every]
    factors = [left_parts(jnp.transpose(upper[f])) for f in every]
    parts = [right_parts(lower[f]) for f in every]
    for i in range(2):
        cut = i * TILE
        after = products(
            [[p[cut:cut + TILE] for p in factors[f]] for f in every],
            [[p[:, cut:] for p in parts[f]] for f in every],
        )
        for f in every:
            value = corner[i] - after[f]
            block = value[:, :TILE] + ridge[f][i]
            if i == 0:
                own(work, f)[...] = block
                scratch[f, 0] = value[:, TILE:]
            else:
                scratch[f, 1] = block
    later = [jnp.concatenate([weights[f], both[f][TILE:]], 1) for f in every]
    side_step(0, [lefts[f, 0] for f in every], [rights[f, 0] for f in every], later)
    final = products(
        [left_parts(jnp.transpose(lefts[f, 0])) for f in every], [right_parts(v) for v in later]
    )
    for f in every:
        wide[f, 0, :, TILE:] = final[f]
    later = [more[f][TILE:] for f in every]
    side_step(1, [lefts[f, 1] for f in every], [rights[f, 1] for f in every], later)
    final = products(
        [left_parts(jnp.transpose(lefts[f, 1])) for f in every], [right_parts(v) for v in later]
    )
    for f in every:
        wide[f, 1, :, 2 * TILE:] = final[f]

    eliminate(work, old, flat, turned, fits)
    left = [lower_part(own(old, f)[...]) for f in every]
    right = [lower_part(own(work, f)[...]) for f in every]
    both = products(
        [left_parts(jnp.concatenate([left[f], right[f]], 0)) for f in every],
        [right_parts(scratch[f, 0]) for f in every],
    )
    later = [both[f][TILE:] for f in every]
    parts = [right_parts(v) for v in later]
    after = products([left_parts(jnp.transpose(both[f][:TILE])) for f in every], parts)
    for f in every:
        own(work, f)[...] = scratch[f, 1] - after[f]
    side_step(2, left, right, later)
    final = products([left_parts(jnp.transpose(left[f])) for f in every], parts)
    for f in every:
        wide[f, 2, :, 3 * TILE:] = final[f]
    eliminate(work, old, flat, turned, fits)
    left = [lower_part(own(old, f)[...]) for f in every]
    right = [lower_part(own(work, f)[...]) for f in every]
    side_step(3, left, right, None)
    for k in reversed(range(TILES - 1)):
        lo, hi = k * TILE, (k + 1) * TILE
        known = [right_parts(jnp.transpose(wide[f, k, :, hi:])) for f in every]
        known = products([left_parts(rhs[f, :, hi:]) for f in every], known)
        for f in every:
            rhs[f, :, lo:hi] = rhs[f, :, lo:hi] - known[f]
    for f in every:
        place_tiles(out, f, [rhs[f, :, t * TILE:(t + 1) * TILE] for t in range(TILES)])


def predict_kernel(pairs, place, mine, other, centre, padded, out):
    odd = place[0] == 1
    rows = []
    for f in range(HALF):
        rows.append(jnp.where(odd, other[f], mine[f]))
    for f in range(HALF):
        rows.append(jnp.where(odd, mine[f], other[f]))
    if pairs:
        upper = iota(rows[0].shape, 0) < TRAITS // 2
        second = place[1] == 1
        halves = [[], []]
        for s in range(0, SLOTS, 2):
            a, b = rows[s], rows[s + 1]
            turned_a, turned_b = (pltpu.roll(v, TRAITS // 2, 0) for v in (a, b))
            low, high = jnp.where(upper, a, turned_b), jnp.where(upper, turned_a, b)
            halves[0].append(jnp.where(second, high, low))
            halves[1].append(jnp.where(second, low, high))
        rows = halves[0] + halves[1]
    weights = jnp.concatenate(rows, 0)
    count = weights.shape[0]
    shift = jnp.sum(weights * centre[0:1, :], axis=1, keepdims=True)
    parts = [part.astype(jnp.float32) for part in split_three(weights)]
    product = dot_bf16(jnp.concatenate(parts, 0).astype(jnp.bfloat16), padded[...])
    total = product[0:count] + product[count:2 * count] + product[2 * count:3 * count] - shift
    if pairs:
        out[0] = total[:count // 2]
        out[1] = total[count // 2:]
    else:
        out[...] = total


def stack_kernel(pairs, per_share, place, mine, other, stats, masked, present, folds, out):
    first = place[1] * per_share
    if pairs:
        second = place[1] == 1
        levels = jnp.concatenate(
            [jnp.where(second, other[...], mine[...]), jnp.where(second, mine[...], other[...])], 0
        )
    else:
        levels = mine[...]
    count, samples = levels.shape
    height, width = out.shape
    present = present[...]
    scaled = (masked[...] - present * stats[:, 0:1]) / stats[:, 1:2]
    pick = iota((count, TRAITS), 1) == first + iota((count, TRAITS), 0) % per_share
    spread = dot_bf16(
        jnp.where(pick, 1.0, 0.0).astype(jnp.bfloat16), present.astype(jnp.bfloat16)
    )
    masks = [
        (spread * jnp.where(folds[...] == k, 1.0, 0.0)).astype(jnp.bfloat16) for k in range(FOLDS)
    ]
    right = split_three(jnp.concatenate([levels, scaled], 0))[:2]
    none = jnp.zeros((width - FOLDS * count, samples), jnp.bfloat16)
    left = [
        jnp.concatenate([part * mask for mask in masks] + [none], 0)
        for part in split_three(levels)[:2]
    ]
    full = dot_bf16(right[1], left[0], NT) + dot_bf16(
        jnp.concatenate([right[0], right[0]], 1), jnp.concatenate([left[1], left[0]], 1), NT
    )
    row, col = iota(full.shape, 0), iota(full.shape, 1)
    trait = jnp.where(row < count, row % per_share, row - count - first)
    full = jnp.where(trait == col % per_share, full, 0.0)
    shape = (height, full.shape[0])
    level, source = iota(shape, 0), iota(shape, 1)
    slot = source // per_share
    group = jnp.where(slot % SLOTS < FITS, slot // SLOTS * FITS + slot % SLOTS, height)
    group = jnp.where(source < count, group, count // per_share // SLOTS * FITS)
    out[...] = dot(jnp.where(level == group, 1.0, 0.0), full)
    ones = jnp.ones((16, samples), jnp.bfloat16)
    squares = split_three(levels * levels)
    energy = dot_bf16(ones, squares[1], NT) + dot_bf16(ones, squares[0], NT)
    last = count // per_share // SLOTS * FITS + 1
    out[last:last + 1, 0:count] = energy[0:1, :]


def scale_kernel(per_share, blocks, samples, total, gram, cross):
    height, width = total.shape
    count = blocks * SLOTS * per_share
    levels = blocks * FITS
    value = total[...]
    energy = jnp.broadcast_to(value[levels + 1:levels + 2, 0:count], (height, count))
    level, column = iota((height, count), 0), iota((height, count), 1) // per_share
    group = jnp.where(column % SLOTS < FITS, column // SLOTS * FITS + column % SLOTS, height)
    shape = (count, width)
    source, target = iota(shape, 0), iota(shape, 1)
    by_row = dot(
        jnp.where(level == group, energy, 0.0),
        jnp.where(source % per_share == target % per_share, 1.0, 0.0),
    )
    by_column = dot(energy, jnp.where(source == target % count, 1.0, 0.0))
    root_row = jnp.where(
        iota((height, width), 0) < levels, jnp.sqrt(by_row / samples + 1e-06), 1.0
    )
    root_column = jnp.sqrt(by_column / samples + 1e-06)
    value = value / root_row / root_column * (FOLDS / samples)
    turned = jnp.transpose(value)
    shape = (FOLDS * 8, width)
    line, column = iota(shape, 0), iota(shape, 1)
    chosen = jnp.logical_and(line // 8 == column // count, line % 8 == column % per_share)
    products = jnp.where(chosen, jnp.broadcast_to(value[levels:levels + 1, :], shape), 0.0)
    shape = (width, TILE)
    slot, target = iota(shape, 0) % count // per_share, iota(shape, 1)
    group = jnp.where(slot % SLOTS < FITS, slot // SLOTS * FITS + slot % SLOTS, -1)
    products = dot(products, jnp.where(group == target, 1.0, 0.0))
    for k in range(FOLDS):
        cross[k] = products[8 * k:8 * k + per_share, 0:levels]
        for l in range(levels):
            row = k * count + (l // FITS * SLOTS + l % FITS) * per_share
            gram[k, l] = turned[row:row + per_share, 0:levels]


def swap(value, axis, mask):
    size = lax.axis_size(axis)
    return lax.ppermute(value, axis, [(i, i ^ mask) for i in range(size)])


def masks_of(axis):
    size, mask, found = lax.axis_size(axis), 1, []
    while mask < size:
        found.append(mask)
        mask *= 2
    return found


def sum_over(value, axis):
    for mask in masks_of(axis):
        value = value + swap(value, axis, mask)
    return value


def body(genotypes, traits, observed, fold_index):
    local_rows, markers = genotypes.shape
    sample_devices = lax.axis_size("samp")
    block_devices = lax.axis_size("blk")
    samples = local_rows * sample_devices
    all_markers = markers * block_devices
    width = -(-markers // TILE) * TILE
    assert width == TILES * TILE and markers + 3 <= width
    per_share = TRAITS // block_devices
    pairs = block_devices == 2
    f32 = functools.partial(jax.ShapeDtypeStruct, dtype=jnp.float32)
    position, block = lax.axis_index("samp"), lax.axis_index("blk")
    odd = position % 2
    late = position // 2 % 2
    place = jnp.stack([odd, block, late]).astype(jnp.int32)
    present = observed.T.astype(jnp.float32)
    masked = present * traits.T

    whole = lambda shape: pl.BlockSpec(shape, lambda _: (0, 0))
    packed, padded = pl.pallas_call(
        functools.partial(gram_kernel, markers),
        grid=(1,),
        out_shape=[
            f32((2 * HALF_ROWS, TILE)),
            jax.ShapeDtypeStruct((width, local_rows), jnp.bfloat16),
        ],
        in_specs=[whole((width, local_rows)), whole(masked.shape), whole(present.shape)],
        out_specs=[whole((2 * HALF_ROWS, TILE)), whole((width, local_rows))],
        compiler_params=pltpu.CompilerParams(vmem_limit_bytes=VMEM_BYTES),
        name="local_gram",
    )(genotypes.T, masked, present)
    quarters = packed.reshape(2, 2, HALF_ROWS // 2, TILE)
    up = odd == 1
    keep = jnp.where(up, quarters[:, 1], quarters[:, 0])
    value = keep + swap(jnp.where(up, quarters[:, 0], quarters[:, 1]), "samp", 1)
    keep = jnp.where(late == 1, value[1], value[0])
    value = keep + swap(jnp.where(late == 1, value[0], value[1]), "samp", 2)
    for mask in masks_of("samp")[2:]:
        value = value + swap(value, "samp", mask)
    other = swap(value, "samp", 1)
    half = jnp.concatenate([jnp.where(up, other, value), jnp.where(up, value, other)], 0)
    theirs = swap(half, "samp", 2)

    penalties = [all_markers * (1.0 - h) / h for h in HERITABILITY]
    penalties = penalties + [penalties[-1]] * (SLOTS - len(penalties))
    penalty = jnp.where(
        odd == 1,
        jnp.array(penalties[HALF:], jnp.float32),
        jnp.array(penalties[:HALF], jnp.float32),
    )
    square = (HALF, TILE, TILE)
    blocks = [pltpu.VMEM((HALF * TILE, TILE), jnp.float32)] * 2
    turns = [pltpu.VMEM((2, (HALF + 1) * STEP, TILE), jnp.float32)] * 2
    started = call(
        functools.partial(first_kernel, samples, markers),
        [f32((HALF, 2, TILE, TILE)), f32((HALF, 2, TILE, TILE)), f32(square), f32(square)],
        ["smem", "smem", "vmem"],
        blocks + turns,
        "first_fits",
        cost=pl.CostEstimate(flops=4 * 10**9, bytes_accessed=2**21, transcendentals=0),
    )(penalty, place, half)
    weights, stats, centre = call(
        functools.partial(second_kernel, samples, markers),
        [f32((HALF, TRAITS, width)), f32((TRAITS, TILE)), f32((8, width))],
        ["smem", "smem"] + ["vmem"] * 6,
        [
            pltpu.VMEM((HALF, TILES, TILE, width), jnp.float32),
            *blocks,
            *turns,
            pltpu.VMEM((HALF, TRAITS, width), jnp.float32),
            pltpu.VMEM((HALF, 2, TILE, TILE), jnp.float32),
        ],
        "second_fits",
    )(penalty, place, half, theirs, *started)
    other = swap(weights, "samp", 1)

    count = SLOTS * TRAITS
    shape = (2, count // 2, local_rows) if pairs else (count, local_rows)
    predicted = call(
        functools.partial(predict_kernel, pairs),
        f32(shape),
        ["smem", "vmem", "vmem", "vmem", "vmem"],
        [],
        "predictions",
    )(place, weights, other, centre, padded)
    if pairs:
        mine, theirs = predicted[0], swap(predicted[1], "blk", 1)
    else:
        shares = predicted.reshape(SLOTS, block_devices, per_share, local_rows)
        shares = lax.all_to_all(shares, "blk", split_axis=1, concat_axis=0, tiled=True)
        mine = theirs = shares.reshape(count, local_rows)

    levels = block_devices * FITS
    height = -(-(levels + 2) // 8) * 8
    lanes = -(-FOLDS * count // TILE) * TILE
    products = call(
        functools.partial(stack_kernel, pairs, per_share),
        f32((height, lanes)),
        ["smem"] + ["vmem"] * 6,
        [],
        "stacking",
    )(place, mine, theirs, stats, masked, present, fold_index[None, :])
    products = sum_over(products, "samp")
    gram, cross = call(
        functools.partial(scale_kernel, per_share, block_devices, samples),
        [f32((FOLDS, levels, per_share, levels)), f32((FOLDS, per_share, levels))],
        ["vmem"],
        [],
        "standardize",
    )(products)
    return gram.transpose(2, 0, 1, 3), cross.transpose(1, 0, 2)


def solution(mesh):
    in_specs = (P("samp", "blk"), P("samp", None), P("samp", None), P("samp"))
    out_specs = (P("blk", None, None, None), P("blk", None, None))
    return jax.shard_map(body, mesh=mesh, in_specs=in_specs, out_specs=out_specs, check_vma=False)
```
